512 devices in a mesh: band: 4 (over y_lo, core), stn: 128 (over z, y_hi, x).
Axes of the slice: x: 4, y: 4 (y_hi: 2, y_lo: 2; y = y_hi * 2 + y_lo), z: 16, core: 2. Of those that a mesh axis runs over, the one named last changes fastest.
Arguments:
- voltages: bfloat16 [2, 512, 2, 192, 1408], P(None, 'stn', None, 'band'), may hold values from -6 to 6
- station_ok: int32 [512], replicated, may hold values 0 or 1
- delays: int32 [512, 512], replicated, may hold values from 0 to 32767
Outputs:
- beam_power: bfloat16 [512, 3, 36864], P(('band', 'stn'))
The draws below stay inside these ranges and needn't reach their ends.
All inputs are finite; a program needn't handle non-finite values.
Results may differ from the reference program's by a relative error of at most 0.0061.
Values may be sent and summed in bfloat16 or wider, within the bound.
A program may use at most 128 MiB of HBM per device.

```python
import math
import jax
import jax.numpy as jnp
from jax import lax

STATIONS = 512
POLS = 2
CH = 192
BEAMS = 512
FINE = 256
TAPS = 4
FRAMES = 3
KEEP = 192
SAMP = 1408


def place_ends(values, own_key, low, high):
    longest = values.shape.index(max(values.shape))
    spots = []
    for shift in (0, 1):
        where = [jax.random.randint(jax.random.fold_in(own_key, axis), (), 0, length) for axis, length in enumerate(values.shape)]
        where[longest] = (where[longest] + shift) % values.shape[longest]
        spots.append(tuple(where))
    return values.at[spots[0]].set(low).at[spots[1]].set(high)


def levels(rng, extent, shards, least, largest):
    gain, own = 1.0, jax.random.fold_in(rng, 6)
    for position, shards_of in shards:
        steps = jnp.exp(jax.random.uniform(jax.random.fold_in(own, position), (shards_of,), jnp.float32, least / len(shards), largest / len(shards)))
        gain = gain * jnp.repeat(steps, extent[position] // shards_of).reshape([-1 if axis == position else 1 for axis in range(len(extent))])
    return gain


def normal_values(stream_key, dims, spread, bound, split=(), kind=jnp.bfloat16):
    values = spread * jax.random.normal(stream_key, dims, jnp.float32)
    if split:
        values = values * levels(stream_key, dims, split, -0.22, 0.18)
    return jnp.clip(values, -bound, bound).astype(kind)


def setup_inputs(seed: int = 0) -> dict:
    key_of = jax.random.split(jax.random.key(seed), 4)
    return {
        "voltages": normal_values(key_of[0], (2, STATIONS, POLS, CH, SAMP), 1.0, 6.0, ((1, 128), (3, 4))),
        "station_ok": place_ends((jax.random.randint(key_of[1], (STATIONS,), 0, 8) < 7).astype(jnp.int32), jax.random.fold_in(key_of[1], 1), 0, 1),
        "delays": place_ends(jax.random.randint(key_of[2], (STATIONS, BEAMS), 0, 32768), jax.random.fold_in(key_of[2], 1), 0, 32767).astype(jnp.int32),
    }


phase_period = 32768

def prototype():
    length = TAPS * FINE
    sample_index = jnp.arange(length, dtype=jnp.float32)
    centred = (sample_index - (length - 1) / 2.0) / FINE
    window = 0.5 - 0.5 * jnp.cos(2.0 * jnp.pi * (sample_index + 0.5) / length)
    taper = jnp.sinc(centred) * window
    taper = taper / jnp.sqrt(jnp.sum(taper * taper) / FINE)
    return taper.reshape(TAPS, 4, FINE // 4)

def frames_of(samples):
    quarter = FINE // 4
    blocks = samples.reshape(samples.shape[:-1] + (SAMP // quarter, quarter))
    taper = prototype()
    pieces = []
    for quarter_index in range(4):
        summed = 0.0
        for tap_index in range(TAPS):
            offset = 4 * tap_index + quarter_index
            picked = lax.slice_in_dim(blocks, offset, offset + 3 * (FRAMES - 1) + 1, 3, blocks.ndim - 2)
            summed = summed + picked * taper[tap_index, quarter_index]
        pieces.append(summed)
    return jnp.concatenate(pieces, axis=-1)

def spectrum_table(per_channel):
    sample_index = jnp.arange(FINE, dtype=jnp.int32)
    frequency = (jnp.arange(per_channel, dtype=jnp.int32) - per_channel // 2) % FINE
    turns = sample_index[:, None] * frequency[None, :] % FINE
    phases = 2.0 * jnp.pi * turns.astype(jnp.float32) / FINE
    cosine = jnp.cos(phases) / math.sqrt(FINE)
    sine_part = jnp.sin(phases) / math.sqrt(FINE)
    from_real = jnp.stack([cosine, -sine_part], axis=1)
    from_imag = jnp.stack([sine_part, cosine], axis=1)
    return jnp.stack([from_real, from_imag]).astype(jnp.bfloat16)

def beam_weights(delays, station_ok, channel):
    turns = delays * channel % phase_period
    phases = 2.0 * jnp.pi / phase_period * turns.astype(jnp.float32)
    station_gain = station_ok.astype(jnp.float32) / math.sqrt(STATIONS)
    real_part = (station_gain[:, None] * jnp.cos(phases)).astype(jnp.bfloat16)
    imag_part = (-station_gain[:, None] * jnp.sin(phases)).astype(jnp.bfloat16)
    return jnp.stack([jnp.stack([real_part, imag_part], axis=1), jnp.stack([-imag_part, real_part], axis=1)])

def reference(voltages, station_ok, delays):
    transform = spectrum_table(KEEP).astype(jnp.float32)

    def one_channel(channel):
        series = lax.dynamic_index_in_dim(voltages, channel, 3, False)
        shaped = frames_of(series).astype(jnp.bfloat16)
        spectra = jnp.einsum('rspfn,rnok->spfok', shaped.astype(jnp.float32), transform).astype(jnp.bfloat16)
        weight = beam_weights(delays, station_ok, channel)
        formed = jnp.einsum('rsob,spfrk->obpfk', weight.astype(jnp.float32), spectra.astype(jnp.float32))
        detected = lax.optimization_barrier(jnp.sum(formed * formed, axis=(0, 2)))
        return detected.astype(jnp.bfloat16)
    powers = lax.map(one_channel, jnp.arange(CH, dtype=jnp.int32))
    return jnp.transpose(powers, (1, 2, 0, 3)).reshape(BEAMS, FRAMES, CH * KEEP)
```

```python
import math

import jax
import jax.numpy as jnp
import numpy as np
from jax import lax
from jax.experimental import pallas as pl
from jax.experimental.pallas import tpu as pltpu
from jax.sharding import PartitionSpec as P

STATIONS = 512
BEAMS = 512
FINE = 256
TAPS = 4
FRAMES = 3
KEEP = 192
HOP = 192
SAMP = 1408
PERIOD = 32768
MESH = pl.DeviceIdType.MESH
VMEM = pltpu.VMEM

BANDS = 4
RINGS = 16
PLANE = 8
STN = RINGS * PLANE
CHANS = 48
PER_Z = CHANS // RINGS
WORKERS = 7
LANES = 128
HALF = 64
ROWS = 2 * STATIONS
DESKS = BANDS * PLANE
SENDERS = RINGS - RINGS // PLANE


def taper_table():
    length = TAPS * FINE
    at = np.arange(length, dtype=np.float64)
    window = 0.5 - 0.5 * np.cos(2.0 * np.pi * (at + 0.5) / length)
    taper = np.sinc((at - (length - 1) / 2.0) / FINE) * window
    taper = taper / np.sqrt(np.sum(taper * taper) / FINE)
    taper = taper.reshape(TAPS, FINE)
    return np.concatenate([taper, np.pad(taper, ((0, 0), (HALF, HALF)))], axis=1).astype(np.float32)


def spectrum_table():
    n = np.arange(FINE)[:, None]
    q = (np.arange(KEEP)[None, :] - KEEP // 2) % FINE
    phase = 2.0 * np.pi * (n * q % FINE) / FINE
    both = np.stack([np.cos(phase), np.sin(phase)], axis=1) / math.sqrt(FINE)
    both = both.reshape(FINE, 2, 3, 1, HALF)
    return np.broadcast_to(both, (FINE, 2, 3, 2, HALF)).reshape(FINE, 768).astype(np.float32)


def sine_coefficients():
    x = np.cos((np.arange(400) + 0.5) * np.pi / 800) * 0.25
    powers = np.stack([x ** (2 * i + 1) for i in range(5)], axis=1)
    return [float(v) for v in np.linalg.lstsq(powers, np.sin(2 * np.pi * x), rcond=None)[0]]


SINE = sine_coefficients()


def one_hot(picked, axis, shape):
    other = lax.broadcasted_iota(jnp.int32, shape, 1 - axis)
    return jnp.where(other == picked(lax.broadcasted_iota(jnp.int32, shape, axis)), 1.0, 0.0).astype(jnp.bfloat16)


def dot(a, b, over=((1,), (0,))):
    return lax.dot_general(a, b, (over, ((), ())), preferred_element_type=jnp.float32)


def kernel(
    volts, taper, waves_far, station_ok, delays, out,
    held, waves, table, filtered, spectra, blocks, middle, landed, delays_in, turns, gains, spread, order, regroup, weights,
    share, share_in, mine, mine_in,
    load_v, load_w, load_d, send_z, recv_z, send_x, recv_x, send_a, recv_a, send_b_sem, recv_b,
):
    band, stn = lax.axis_index("band"), lax.axis_index("stn")
    z, j = stn // PLANE, stn % PLANE
    rank = (j + 3 * PLANE - 1 - z) % PLANE
    works = rank < WORKERS
    at = band * PLANE + j
    bf16, f32 = jnp.bfloat16, jnp.float32

    barrier = pltpu.get_barrier_semaphore()

    def greet_column(i, _):
        other = (band, (z + i) % RINGS * PLANE + j)
        pl.semaphore_signal(barrier, inc=1, device_id=other, device_id_type=MESH)
        return 0

    lax.fori_loop(1, RINGS, greet_column, 0)

    def greet_plane(i, _):
        to = (at + i) % DESKS
        other = (to // PLANE, z * PLANE + to % PLANE)
        pl.semaphore_signal(barrier, inc=1, device_id=other, device_id_type=MESH)
        return 0

    lax.fori_loop(1, DESKS, greet_plane, 0)

    pltpu.make_async_copy(waves_far, waves, load_w).start()
    for s in range(4):
        pltpu.make_async_copy(volts.at[:, s], held.at[:, s], load_v.at[s]).start()
    pltpu.make_async_copy(delays, delays_in, load_d).start()

    low = lax.broadcasted_iota(jnp.int32, (64, 384), 1) % LANES < HALF

    def table_step(i, _):
        at = pl.multiple_of(i * 64, 64)
        cosine, sine = waves[pl.ds(at, 64), :384], waves[pl.ds(at, 64), 384:]
        for p in range(2):
            own = low if p == 0 else jnp.logical_not(low)
            c, s = jnp.where(own, cosine, 0.0), jnp.where(own, sine, 0.0)
            table[pl.ds(512 * p + at, 64), :384] = c.astype(bf16)
            table[pl.ds(512 * p + at, 64), 384:] = (-s).astype(bf16)
            table[pl.ds(512 * p + 256 + at, 64), :384] = s.astype(bf16)
            table[pl.ds(512 * p + 256 + at, 64), 384:] = c.astype(bf16)
        return 0

    pltpu.make_async_copy(waves_far, waves, load_w).wait()
    lax.fori_loop(0, 4, table_step, 0)

    def filter_station(s, _):
        pltpu.make_async_copy(volts.at[:, s], held.at[:, s], load_v.at[s]).wait()

        def filter_step(cb, _):
            for p in range(2):
                for r in range(2):
                    v = held[r, s, p, pl.ds(pl.multiple_of(cb * 16, 16), 16), :].astype(f32)
                    for f in range(FRAMES):
                        total = None
                        for m in range(TAPS):
                            start = f * HOP + m * FINE
                            if f == 1:
                                term = v[:, start - HALF : start + FINE + HALF] * taper[m : m + 1, FINE:]
                            else:
                                term = v[:, start : start + FINE] * taper[m : m + 1, :FINE]
                            total = term if total is None else total + term
                        if f == 1:
                            total = total[:, HALF : HALF + FINE]
                        at = pl.multiple_of((f * 3 + cb) * 64 + s * 16, 16)
                        lanes = slice((p * 2 + r) * FINE, (p * 2 + r + 1) * FINE)
                        filtered[pl.ds(at, 16), lanes] = total.astype(bf16)
            return 0

        lax.fori_loop(0, 3, filter_step, 0)
        return 0

    lax.fori_loop(0, 4, filter_station, 0)

    def transform(f):
        y = dot(filtered[f * 192 : (f + 1) * 192, :], table[...])
        for cb in range(3):
            for s in range(4):
                for part in range(6):
                    ri, g = part // 3, part % 3
                    start = ((f * CHANS + cb * 16) * 3 + g) * 8 + ri * 4 + s
                    spectra[pl.ds(start, 16, stride=24), :] = y[
                        cb * 64 + s * 16 : cb * 64 + s * 16 + 16, part * LANES : (part + 1) * LANES
                    ]

    def pack(t):
        def units(f, zz, first, last):
            start = pl.multiple_of(f * CHANS * 24 + zz * 72 + first * 8, 8)
            return spectra[pl.ds(start, (last - first) * 8), :]

        def pack_step(zz, _):
            if t == 0:
                rows = [units(0, zz, 0, 9), units(1, zz, 0, 5)]
            else:
                rows = [units(1, zz, 5, 9), units(2, zz, 0, 9), jnp.zeros((8, LANES), f32)]
            rows = jnp.concatenate(rows, axis=0).astype(bf16)
            blocks[t, zz] = rows.reshape(WORKERS, 16, LANES)
            return 0

        lax.fori_loop(0, RINGS, pack_step, 0)

    def send_along(t):
        def send_one(slot, zz):
            pltpu.make_async_remote_copy(
                src_ref=blocks.at[t, zz],
                dst_ref=middle.at[t, slot],
                send_sem=send_z,
                recv_sem=recv_z.at[t, slot // 4],
                device_id=(band, zz * PLANE + j),
                device_id_type=MESH,
            ).start()

        def send_two(h, _):
            send_one(2 * h, (z + 1 + h) % RINGS)
            send_one(2 * h + 1, (z + RINGS - 1 - h) % RINGS)
            return 0

        lax.fori_loop(0, RINGS // 2 - 1, send_two, 0)
        send_one(RINGS - 2, (z + RINGS // 2) % RINGS)

    def pass_on(t, k, source, target):
        @pl.when(k == rank)
        def _():
            pltpu.make_async_copy(source, target, recv_x.at[t]).start()

        @pl.when(k != rank)
        def _():
            pltpu.make_async_remote_copy(
                src_ref=source,
                dst_ref=target,
                send_sem=send_x,
                recv_sem=recv_x.at[t],
                device_id=(band, z * PLANE + (z + 1 + k) % PLANE),
                device_id_type=MESH,
            ).start()

    def pass_own(t):
        def one(i, _):
            k = (j + i) % WORKERS
            pass_on(t, k, blocks.at[t, z, k], landed.at[t, j, RINGS - 1])
            return 0

        lax.fori_loop(0, WORKERS, one, 0)

    def pass_group(t, group):
        slots = slice(4 * group, min(4 * group + 4, RINGS - 1))
        slots = pl.ds(slots.start, slots.stop - slots.start)
        arrived = middle.at[t, slots]
        pltpu.make_async_copy(arrived, arrived, recv_z.at[t, group]).wait()

        def one(i, _):
            k = (j + i) % WORKERS
            pass_on(t, k, middle.at[t, slots, k], landed.at[t, j, slots])
            return 0

        lax.fori_loop(0, WORKERS, one, 0)

    transform(0)
    transform(1)
    pack(0)
    pl.semaphore_wait(barrier, RINGS - 1 + DESKS - 1)
    send_along(0)
    pass_own(0)
    transform(2)
    pack(1)
    send_along(1)
    pass_own(1)

    pltpu.make_async_copy(delays, delays_in, load_d).wait()

    def station(k):
        slot = (k >> 3) & 15
        ahead = ((slot >> 1) + 1) * (1 - 2 * (slot & 1))
        ahead = jnp.where(slot == RINGS - 1, 0, ahead)
        return ((((z + RINGS - ahead) & 15) * PLANE) + (k >> 7)) * 4 + (k & 3)

    spread[...] = one_hot(station, 1, (STATIONS, ROWS))
    order[...] = one_hot(lambda b: ((b >> 3) & 3) * 128 + (b >> 5) * 8 + (b & 7), 0, (BEAMS, BEAMS))
    for part in range(2):
        d = delays_in[...]
        d = (d >> 8 if part else d & 255).astype(f32).astype(bf16)
        d = dot(order[...], d, ((1,), (1,))).astype(bf16)
        d = dot(d, spread[...])
        if part:
            turns[...] += d * 256.0
        else:
            turns[...] = d
    ok = jnp.broadcast_to(station_ok[...].astype(f32), (8, STATIONS)).astype(bf16)
    gains[...] = dot(ok, spread[...]) * (1.0 / math.sqrt(STATIONS))

    def place(k):
        after = ((k & 15) + RINGS - 1 - j) & 15
        return jnp.where((after & 7) == 7, -1, (after - (after >> 3)) * DESKS + (k >> 4))

    regroup[...] = one_hot(place, 0, (BEAMS, SENDERS * DESKS))

    imag = (lax.broadcasted_iota(jnp.int32, (16, ROWS), 1) >> 2) & 1
    quarter = imag.astype(f32) * -0.25
    first_channel = (band * CHANS + z * PER_Z).astype(f32)

    def weight_step(i, _):
        rows = pl.ds(pl.multiple_of(i * 16, 16), 16)
        x = turns[rows, :]
        gain = jnp.concatenate([gains[...]] * 2, axis=0)
        for c in range(PER_Z):
            turn = x * ((first_channel + float(c)) * (1.0 / PERIOD)) + quarter
            turn = turn - jnp.floor(turn + 0.5)
            a = 0.25 - jnp.abs(turn)
            square = a * a
            value = SINE[4]
            for coefficient in SINE[3::-1]:
                value = value * square + coefficient
            weights[c, rows, :] = (value * a * gain).astype(bf16)
        return 0

    for group in range(4):
        lax.fori_loop(group * 8, group * 8 + 8, weight_step, 0)
        pass_group(0, group)
    pass_group(1, 0)
    pass_group(1, 1)

    upper = lax.broadcasted_iota(jnp.int32, (1, 8, LANES), 1) < 4
    sign = jnp.where(upper, 1.0, -1.0)
    left = lax.broadcasted_iota(jnp.int32, (BEAMS, LANES), 1) < HALF

    after = (z + RINGS - 1 - j) % RINGS
    slot = after - after // PLANE

    def form(t):
        @pl.when(works)
        def _():
            pltpu.make_async_copy(landed.at[t], landed.at[t], recv_x.at[t]).wait()
            x = landed[t].reshape(STN, 16, LANES).astype(f32)
            powers = []
            for h in range(2):
                unit = 2 * (t * WORKERS + rank) + h
                c = (unit // 3) % 3
                for_real = x[:, 8 * h : 8 * h + 8]
                for_imag = pltpu.roll(for_real, 4, 1) * sign
                both = jnp.concatenate([for_real.reshape(ROWS, LANES), for_imag.reshape(ROWS, LANES)], axis=1)
                y = dot(weights[c], both.astype(bf16))
                y = y[:, :LANES] * y[:, :LANES] + y[:, LANES:] * y[:, LANES:]
                powers.append(y + pltpu.roll(y, HALF, 1))
            y = jnp.where(left, powers[0], powers[1]).astype(bf16)
            share[t] = y.reshape(RINGS, DESKS, LANES)

            def send_a_step(i, _, t=t):
                zz = (z + i) % RINGS
                pltpu.make_async_remote_copy(
                    src_ref=share.at[t, zz],
                    dst_ref=share_in.at[t, slot],
                    send_sem=send_a,
                    recv_sem=recv_a.at[t],
                    device_id=(band, zz * PLANE + j),
                    device_id_type=MESH,
                ).start()
                return 0

            lax.fori_loop(1, RINGS, send_a_step, 0)
            pltpu.make_async_copy(share.at[t, z], share_in.at[t, slot], recv_a.at[t]).start()

    form(0)
    pass_group(1, 2)
    pass_group(1, 3)
    form(1)

    for t in range(2):
        pltpu.make_async_copy(share_in.at[t], share_in.at[t], recv_a.at[t]).wait()
        moved = dot(regroup[...], share_in[t].reshape(SENDERS * DESKS, LANES))
        mine[t] = moved.astype(bf16).reshape(DESKS, RINGS, LANES)

        def send_b(i, t=t):
            to = (at + i) % DESKS
            pltpu.make_async_remote_copy(
                src_ref=mine.at[t, to],
                dst_ref=mine_in.at[t, at],
                send_sem=send_b_sem,
                recv_sem=recv_b.at[t],
                device_id=(to // PLANE, z * PLANE + to % PLANE),
                device_id_type=MESH,
            ).start()

        def send_b_step(n, _, send_b=send_b):
            for i in range(5):
                send_b(5 * n + 1 + i)
            return 0

        lax.fori_loop(0, 6, send_b_step, 0)
        send_b(DESKS - 1)
        pltpu.make_async_copy(mine.at[t, at], mine_in.at[t, at], recv_b.at[t]).start()

    for t in range(2):
        pltpu.make_async_copy(mine_in.at[t], mine_in.at[t], recv_b.at[t]).wait()
    width = PER_Z * KEEP
    row = lax.broadcasted_iota(jnp.int32, (RINGS, LANES), 0)
    for b in range(BANDS):
        wide = []
        for t in range(2):
            turned = [mine_in[t, b * PLANE + place].astype(f32) for place in range(PLANE)]
            for step in (1, 2, 4):
                turned = [
                    jnp.where((row & step) > 0, turned[(i + step) % PLANE], turned[i]) for i in range(PLANE)
                ]
            wide += turned[1:]
        wide = jnp.concatenate(wide, axis=1)
        for f in range(FRAMES):
            out[f, b] = wide[:, f * width : (f + 1) * width].astype(bf16)

    some = mine.at[:, pl.ds(0, DESKS - 1)]
    pltpu.make_async_copy(some, some, send_b_sem).wait()
    some = blocks.at[:, pl.ds(0, RINGS - 1)]
    pltpu.make_async_copy(some, some, send_z).wait()

    @pl.when(works)
    def _():
        some = blocks.at[:, :, pl.ds(0, WORKERS - 1)]
        pltpu.make_async_copy(some, some, send_x).wait()
        some = share.at[:, pl.ds(0, RINGS - 1)]
        pltpu.make_async_copy(some, some, send_a).wait()

    @pl.when(jnp.logical_not(works))
    def _():
        pltpu.make_async_copy(blocks, blocks, send_x).wait()


def local(voltages, station_ok, delays):
    in_vmem, anywhere = pl.BlockSpec(memory_space=VMEM), pl.BlockSpec(memory_space=pl.ANY)
    bf16, f32 = jnp.bfloat16, jnp.float32
    dma = pltpu.SemaphoreType.DMA
    formed = pl.pallas_call(
        kernel,
        name="beams",
        out_shape=jax.ShapeDtypeStruct((FRAMES, BANDS, RINGS, PER_Z * KEEP), bf16),
        in_specs=[anywhere, in_vmem, anywhere, in_vmem, anywhere],
        out_specs=in_vmem,
        scratch_shapes=[
            VMEM((2, 4, 2, CHANS, SAMP), bf16),
            VMEM((FINE, 768), f32),
            VMEM((1024, 768), bf16),
            VMEM((FRAMES * CHANS * 4, 1024), bf16),
            VMEM((FRAMES * CHANS * 24, LANES), f32),
            VMEM((2, RINGS, WORKERS, 16, LANES), bf16),
            VMEM((2, RINGS - 1, WORKERS, 16, LANES), bf16),
            VMEM((2, PLANE, RINGS, 16, LANES), bf16),
            VMEM((STATIONS, BEAMS), jnp.int32),
            VMEM((BEAMS, ROWS), f32),
            VMEM((8, ROWS), f32),
            VMEM((STATIONS, ROWS), bf16),
            VMEM((BEAMS, BEAMS), bf16),
            VMEM((BEAMS, SENDERS * DESKS), bf16),
            VMEM((PER_Z, BEAMS, ROWS), bf16),
            VMEM((2, RINGS, DESKS, LANES), bf16),
            VMEM((2, SENDERS, DESKS, LANES), bf16),
            VMEM((2, DESKS, RINGS, LANES), bf16),
            VMEM((2, DESKS, RINGS, LANES), bf16),
            dma((4,)), dma, dma, dma, dma((2, 4)), dma, dma((2,)), dma, dma((2,)), dma, dma((2,)),
        ],
        compiler_params=pltpu.CompilerParams(
            collective_id=0, has_side_effects=True, vmem_limit_bytes=60 * 2**20
        ),
    )(voltages, jnp.asarray(taper_table()), jnp.asarray(spectrum_table()), station_ok.reshape(1, STATIONS), delays)
    return formed.reshape(1, FRAMES, BANDS * CHANS * KEEP)


def solution(mesh):
    placed = (P(None, "stn", None, "band", None), P(), P())
    return jax.shard_map(
        local, mesh=mesh, in_specs=placed, out_specs=P(("band", "stn"), None, None), check_vma=False
    )
```

```python
import math

import jax
import jax.numpy as jnp
import numpy as np
from jax import lax
from jax.experimental import pallas as pl
from jax.experimental.pallas import tpu as pltpu
from jax.sharding import PartitionSpec as P

STATIONS = 512
BEAMS = 512
FINE = 256
TAPS = 4
FRAMES = 3
KEEP = 192
HOP = 192
SAMP = 1408
PERIOD = 32768
MESH = pl.DeviceIdType.MESH
VMEM = pltpu.VMEM

BANDS = 4
RINGS = 16
PLANE = 8
STN = RINGS * PLANE
CHANS = 48
PER_Z = CHANS // RINGS
WORKERS = 7
LANES = 128
HALF = 64
ROWS = 2 * STATIONS
DESKS = BANDS * PLANE
SENDERS = RINGS - RINGS // PLANE


def taper_table():
    length = TAPS * FINE
    at = np.arange(length, dtype=np.float64)
    window = 0.5 - 0.5 * np.cos(2.0 * np.pi * (at + 0.5) / length)
    taper = np.sinc((at - (length - 1) / 2.0) / FINE) * window
    taper = taper / np.sqrt(np.sum(taper * taper) / FINE)
    taper = taper.reshape(TAPS, FINE)
    return np.concatenate([taper, np.pad(taper, ((0, 0), (HALF, HALF)))], axis=1).astype(np.float32)


def spectrum_table():
    n = np.arange(FINE)[:, None]
    q = (np.arange(KEEP)[None, :] - KEEP // 2) % FINE
    phase = 2.0 * np.pi * (n * q % FINE) / FINE
    both = np.stack([np.cos(phase), np.sin(phase)], axis=1) / math.sqrt(FINE)
    both = both.reshape(FINE, 2, 3, 1, HALF)
    return np.broadcast_to(both, (FINE, 2, 3, 2, HALF)).reshape(FINE, 768).astype(np.float32)


def sine_coefficients():
    x = np.cos((np.arange(400) + 0.5) * np.pi / 800) * 0.25
    powers = np.stack([x ** (2 * i + 1) for i in range(5)], axis=1)
    return [float(v) for v in np.linalg.lstsq(powers, np.sin(2 * np.pi * x), rcond=None)[0]]


SINE = sine_coefficients()


def one_hot(picked, axis, shape):
    other = lax.broadcasted_iota(jnp.int32, shape, 1 - axis)
    return jnp.where(other == picked(lax.broadcasted_iota(jnp.int32, shape, axis)), 1.0, 0.0).astype(jnp.bfloat16)


def dot(a, b, over=((1,), (0,))):
    return lax.dot_general(a, b, (over, ((), ())), preferred_element_type=jnp.float32)


def kernel(
    volts, taper, waves_far, station_ok, delays, out,
    held, waves, table, filtered, spectra, blocks, middle, relay, landed, delays_in, turns, gains, spread, order, regroup, weights,
    share, share_in, mine, mine_in,
    load_v, load_w, load_d, send_z, recv_z, relay_in, relay_out, send_x, recv_x, send_a, recv_a, send_b_sem, recv_b,
):
    band, stn = lax.axis_index("band"), lax.axis_index("stn")
    z, j = stn // PLANE, stn % PLANE
    rank = (j + 3 * PLANE - 1 - z) % PLANE
    works = rank < WORKERS
    at = band * PLANE + j
    bf16, f32 = jnp.bfloat16, jnp.float32

    barrier = pltpu.get_barrier_semaphore()

    def greet_column(i, _):
        other = (band, (z + i) % RINGS * PLANE + j)
        pl.semaphore_signal(barrier, inc=1, device_id=other, device_id_type=MESH)
        return 0

    lax.fori_loop(1, RINGS, greet_column, 0)

    def greet_plane(i, _):
        to = (at + i) % DESKS
        other = (to // PLANE, z * PLANE + to % PLANE)
        pl.semaphore_signal(barrier, inc=1, device_id=other, device_id_type=MESH)
        return 0

    lax.fori_loop(1, DESKS, greet_plane, 0)

    pltpu.make_async_copy(waves_far, waves, load_w).start()
    for s in range(4):
        pltpu.make_async_copy(volts.at[:, s], held.at[:, s], load_v.at[s]).start()
    pltpu.make_async_copy(delays, delays_in, load_d).start()

    low = lax.broadcasted_iota(jnp.int32, (64, 384), 1) % LANES < HALF

    def table_step(i, _):
        at = pl.multiple_of(i * 64, 64)
        cosine, sine = waves[pl.ds(at, 64), :384], waves[pl.ds(at, 64), 384:]
        for p in range(2):
            own = low if p == 0 else jnp.logical_not(low)
            c, s = jnp.where(own, cosine, 0.0), jnp.where(own, sine, 0.0)
            table[pl.ds(512 * p + at, 64), :384] = c.astype(bf16)
            table[pl.ds(512 * p + at, 64), 384:] = (-s).astype(bf16)
            table[pl.ds(512 * p + 256 + at, 64), :384] = s.astype(bf16)
            table[pl.ds(512 * p + 256 + at, 64), 384:] = c.astype(bf16)
        return 0

    pltpu.make_async_copy(waves_far, waves, load_w).wait()
    lax.fori_loop(0, 4, table_step, 0)

    def filter_station(s, _):
        pltpu.make_async_copy(volts.at[:, s], held.at[:, s], load_v.at[s]).wait()

        def filter_step(cb, _):
            for p in range(2):
                for r in range(2):
                    v = held[r, s, p, pl.ds(pl.multiple_of(cb * 16, 16), 16), :].astype(f32)
                    for f in range(FRAMES):
                        total = None
                        for m in range(TAPS):
                            start = f * HOP + m * FINE
                            if f == 1:
                                term = v[:, start - HALF : start + FINE + HALF] * taper[m : m + 1, FINE:]
                            else:
                                term = v[:, start : start + FINE] * taper[m : m + 1, :FINE]
                            total = term if total is None else total + term
                        if f == 1:
                            total = total[:, HALF : HALF + FINE]
                        at = pl.multiple_of((f * 3 + cb) * 64 + s * 16, 16)
                        lanes = slice((p * 2 + r) * FINE, (p * 2 + r + 1) * FINE)
                        filtered[pl.ds(at, 16), lanes] = total.astype(bf16)
            return 0

        lax.fori_loop(0, 3, filter_step, 0)
        return 0

    lax.fori_loop(0, 4, filter_station, 0)

    def transform(f):
        y = dot(filtered[f * 192 : (f + 1) * 192, :], table[...])
        for cb in range(3):
            for s in range(4):
                for part in range(6):
                    ri, g = part // 3, part % 3
                    start = ((f * CHANS + cb * 16) * 3 + g) * 8 + ri * 4 + s
                    spectra[pl.ds(start, 16, stride=24), :] = y[
                        cb * 64 + s * 16 : cb * 64 + s * 16 + 16, part * LANES : (part + 1) * LANES
                    ]

    def pack(t):
        def units(f, zz, first, last):
            start = pl.multiple_of(f * CHANS * 24 + zz * 72 + first * 8, 8)
            return spectra[pl.ds(start, (last - first) * 8), :]

        def pack_step(zz, _):
            if t == 0:
                rows = [units(0, zz, 0, 9), units(1, zz, 0, 5)]
            else:
                rows = [units(1, zz, 5, 9), units(2, zz, 0, 9), jnp.zeros((8, LANES), f32)]
            rows = jnp.concatenate(rows, axis=0).astype(bf16)
            blocks[t, zz] = rows.reshape(WORKERS, 16, LANES)
            return 0

        lax.fori_loop(0, RINGS, pack_step, 0)

    def send_along(t):
        def send_one(slot, zz):
            pltpu.make_async_remote_copy(
                src_ref=blocks.at[t, zz],
                dst_ref=middle.at[t, slot],
                send_sem=send_z,
                recv_sem=recv_z.at[t, slot // 4],
                device_id=(band, zz * PLANE + j),
                device_id_type=MESH,
            ).start()

        def send_two(h, _):
            send_one(2 * h, (z + 1 + h) % RINGS)
            send_one(2 * h + 1, (z + RINGS - 1 - h) % RINGS)
            return 0

        pltpu.make_async_remote_copy(
            src_ref=blocks.at[t, (z + RINGS // 2) % RINGS],
            dst_ref=relay.at[t],
            send_sem=send_z,
            recv_sem=relay_in.at[t],
            device_id=(band, (z + quarter_way[t]) % RINGS * PLANE + j),
            device_id_type=MESH,
        ).start()
        lax.fori_loop(0, RINGS // 2 - 1, send_two, 0)

    quarter_way = (RINGS // 4, RINGS - RINGS // 4)

    def second_leg(t):
        pltpu.make_async_copy(relay.at[t], relay.at[t], relay_in.at[t]).wait()
        pltpu.make_async_remote_copy(
            src_ref=relay.at[t],
            dst_ref=middle.at[t, RINGS - 2],
            send_sem=relay_out,
            recv_sem=recv_z.at[t, 3],
            device_id=(band, (z + quarter_way[t]) % RINGS * PLANE + j),
            device_id_type=MESH,
        ).start()

    def pass_on(t, k, source, target):
        @pl.when(k == rank)
        def _():
            pltpu.make_async_copy(source, target, recv_x.at[t]).start()

        @pl.when(k != rank)
        def _():
            pltpu.make_async_remote_copy(
                src_ref=source,
                dst_ref=target,
                send_sem=send_x,
                recv_sem=recv_x.at[t],
                device_id=(band, z * PLANE + (z + 1 + k) % PLANE),
                device_id_type=MESH,
            ).start()

    def pass_own(t):
        def one(i, _):
            k = (j + i) % WORKERS
            pass_on(t, k, blocks.at[t, z, k], landed.at[t, j, RINGS - 1])
            return 0

        lax.fori_loop(0, WORKERS, one, 0)

    def pass_group(t, group):
        slots = slice(4 * group, min(4 * group + 4, RINGS - 1))
        slots = pl.ds(slots.start, slots.stop - slots.start)
        arrived = middle.at[t, slots]
        pltpu.make_async_copy(arrived, arrived, recv_z.at[t, group]).wait()

        def one(i, _):
            k = (j + i) % WORKERS
            pass_on(t, k, middle.at[t, slots, k], landed.at[t, j, slots])
            return 0

        lax.fori_loop(0, WORKERS, one, 0)

    transform(0)
    transform(1)
    pack(0)
    pl.semaphore_wait(barrier, RINGS - 1 + DESKS - 1)
    send_along(0)
    pass_own(0)
    transform(2)
    pack(1)
    send_along(1)
    pass_own(1)

    pltpu.make_async_copy(delays, delays_in, load_d).wait()

    def station(k):
        slot = (k >> 3) & 15
        ahead = ((slot >> 1) + 1) * (1 - 2 * (slot & 1))
        ahead = jnp.where(slot == RINGS - 1, 0, ahead)
        return ((((z + RINGS - ahead) & 15) * PLANE) + (k >> 7)) * 4 + (k & 3)

    spread[...] = one_hot(station, 1, (STATIONS, ROWS))
    order[...] = one_hot(lambda b: ((b >> 3) & 3) * 128 + (b >> 5) * 8 + (b & 7), 0, (BEAMS, BEAMS))
    for part in range(2):
        d = delays_in[...]
        d = (d >> 8 if part else d & 255).astype(f32).astype(bf16)
        d = dot(order[...], d, ((1,), (1,))).astype(bf16)
        d = dot(d, spread[...])
        if part:
            turns[...] += d * 256.0
        else:
            turns[...] = d
    ok = jnp.broadcast_to(station_ok[...].astype(f32), (8, STATIONS)).astype(bf16)
    gains[...] = dot(ok, spread[...]) * (1.0 / math.sqrt(STATIONS))

    def place(k):
        after = ((k & 15) + RINGS - 1 - j) & 15
        return jnp.where((after & 7) == 7, -1, (after - (after >> 3)) * DESKS + (k >> 4))

    regroup[...] = one_hot(place, 0, (BEAMS, SENDERS * DESKS))

    imag = (lax.broadcasted_iota(jnp.int32, (16, ROWS), 1) >> 2) & 1
    quarter = imag.astype(f32) * -0.25
    first_channel = (band * CHANS + z * PER_Z).astype(f32)

    def weight_step(i, _):
        rows = pl.ds(pl.multiple_of(i * 16, 16), 16)
        x = turns[rows, :]
        gain = jnp.concatenate([gains[...]] * 2, axis=0)
        for c in range(PER_Z):
            turn = x * ((first_channel + float(c)) * (1.0 / PERIOD)) + quarter
            turn = turn - jnp.floor(turn + 0.5)
            a = 0.25 - jnp.abs(turn)
            square = a * a
            value = SINE[4]
            for coefficient in SINE[3::-1]:
                value = value * square + coefficient
            weights[c, rows, :] = (value * a * gain).astype(bf16)
        return 0

    for group in range(4):
        lax.fori_loop(group * 8, group * 8 + 8, weight_step, 0)
        if group == 0:
            second_leg(0)
        pass_group(0, group)
    second_leg(1)
    pass_group(1, 0)
    pass_group(1, 1)

    upper = lax.broadcasted_iota(jnp.int32, (1, 8, LANES), 1) < 4
    sign = jnp.where(upper, 1.0, -1.0)
    left = lax.broadcasted_iota(jnp.int32, (BEAMS, LANES), 1) < HALF

    after = (z + RINGS - 1 - j) % RINGS
    slot = after - after // PLANE

    def form(t):
        @pl.when(works)
        def _():
            pltpu.make_async_copy(landed.at[t], landed.at[t], recv_x.at[t]).wait()
            x = landed[t].reshape(STN, 16, LANES).astype(f32)
            powers = []
            for h in range(2):
                unit = 2 * (t * WORKERS + rank) + h
                c = (unit // 3) % 3
                for_real = x[:, 8 * h : 8 * h + 8]
                for_imag = pltpu.roll(for_real, 4, 1) * sign
                both = jnp.concatenate([for_real.reshape(ROWS, LANES), for_imag.reshape(ROWS, LANES)], axis=1)
                y = dot(weights[c], both.astype(bf16))
                y = y[:, :LANES] * y[:, :LANES] + y[:, LANES:] * y[:, LANES:]
                powers.append(y + pltpu.roll(y, HALF, 1))
            y = jnp.where(left, powers[0], powers[1]).astype(bf16)
            share[t] = y.reshape(RINGS, DESKS, LANES)

            def send_a_step(i, _, t=t):
                zz = (z + i) % RINGS
                pltpu.make_async_remote_copy(
                    src_ref=share.at[t, zz],
                    dst_ref=share_in.at[t, slot],
                    send_sem=send_a,
                    recv_sem=recv_a.at[t],
                    device_id=(band, zz * PLANE + j),
                    device_id_type=MESH,
                ).start()
                return 0

            lax.fori_loop(1, RINGS, send_a_step, 0)
            pltpu.make_async_copy(share.at[t, z], share_in.at[t, slot], recv_a.at[t]).start()

    form(0)
    pass_group(1, 2)
    pass_group(1, 3)
    form(1)

    for t in range(2):
        pltpu.make_async_copy(share_in.at[t], share_in.at[t], recv_a.at[t]).wait()
        moved = dot(regroup[...], share_in[t].reshape(SENDERS * DESKS, LANES))
        mine[t] = moved.astype(bf16).reshape(DESKS, RINGS, LANES)

        def send_b(i, t=t):
            to = (at + i) % DESKS
            pltpu.make_async_remote_copy(
                src_ref=mine.at[t, to],
                dst_ref=mine_in.at[t, at],
                send_sem=send_b_sem,
                recv_sem=recv_b.at[t],
                device_id=(to // PLANE, z * PLANE + to % PLANE),
                device_id_type=MESH,
            ).start()

        def send_b_step(n, _, send_b=send_b):
            for i in range(5):
                send_b(5 * n + 1 + i)
            return 0

        lax.fori_loop(0, 6, send_b_step, 0)
        send_b(DESKS - 1)
        pltpu.make_async_copy(mine.at[t, at], mine_in.at[t, at], recv_b.at[t]).start()

    for t in range(2):
        pltpu.make_async_copy(mine_in.at[t], mine_in.at[t], recv_b.at[t]).wait()
    width = PER_Z * KEEP
    row = lax.broadcasted_iota(jnp.int32, (RINGS, LANES), 0)
    for b in range(BANDS):
        wide = []
        for t in range(2):
            turned = [mine_in[t, b * PLANE + place].astype(f32) for place in range(PLANE)]
            for step in (1, 2, 4):
                turned = [
                    jnp.where((row & step) > 0, turned[(i + step) % PLANE], turned[i]) for i in range(PLANE)
                ]
            wide += turned[1:]
        wide = jnp.concatenate(wide, axis=1)
        for f in range(FRAMES):
            out[f, b] = wide[:, f * width : (f + 1) * width].astype(bf16)

    some = mine.at[:, pl.ds(0, DESKS - 1)]
    pltpu.make_async_copy(some, some, send_b_sem).wait()
    pltpu.make_async_copy(relay, relay, relay_out).wait()
    some = blocks.at[:, pl.ds(0, RINGS - 1)]
    pltpu.make_async_copy(some, some, send_z).wait()

    @pl.when(works)
    def _():
        some = blocks.at[:, :, pl.ds(0, WORKERS - 1)]
        pltpu.make_async_copy(some, some, send_x).wait()
        some = share.at[:, pl.ds(0, RINGS - 1)]
        pltpu.make_async_copy(some, some, send_a).wait()

    @pl.when(jnp.logical_not(works))
    def _():
        pltpu.make_async_copy(blocks, blocks, send_x).wait()


def local(voltages, station_ok, delays):
    in_vmem, anywhere = pl.BlockSpec(memory_space=VMEM), pl.BlockSpec(memory_space=pltpu.HBM)
    bf16, f32 = jnp.bfloat16, jnp.float32
    dma = pltpu.SemaphoreType.DMA
    formed = pl.pallas_call(
        kernel,
        name="beams",
        out_shape=jax.ShapeDtypeStruct((FRAMES, BANDS, RINGS, PER_Z * KEEP), bf16),
        in_specs=[anywhere, in_vmem, anywhere, in_vmem, anywhere],
        out_specs=in_vmem,
        scratch_shapes=[
            VMEM((2, 4, 2, CHANS, SAMP), bf16),
            VMEM((FINE, 768), f32),
            VMEM((1024, 768), bf16),
            VMEM((FRAMES * CHANS * 4, 1024), bf16),
            VMEM((FRAMES * CHANS * 24, LANES), f32),
            VMEM((2, RINGS, WORKERS, 16, LANES), bf16),
            VMEM((2, RINGS - 1, WORKERS, 16, LANES), bf16),
            VMEM((2, WORKERS, 16, LANES), bf16),
            VMEM((2, PLANE, RINGS, 16, LANES), bf16),
            VMEM((STATIONS, BEAMS), jnp.int32),
            VMEM((BEAMS, ROWS), f32),
            VMEM((8, ROWS), f32),
            VMEM((STATIONS, ROWS), bf16),
            VMEM((BEAMS, BEAMS), bf16),
            VMEM((BEAMS, SENDERS * DESKS), bf16),
            VMEM((PER_Z, BEAMS, ROWS), bf16),
            VMEM((2, RINGS, DESKS, LANES), bf16),
            VMEM((2, SENDERS, DESKS, LANES), bf16),
            VMEM((2, DESKS, RINGS, LANES), bf16),
            VMEM((2, DESKS, RINGS, LANES), bf16),
            dma((4,)), dma, dma, dma, dma((2, 4)), dma((2,)), dma, dma, dma((2,)), dma, dma((2,)), dma, dma((2,)),
        ],
        compiler_params=pltpu.CompilerParams(
            collective_id=0, has_side_effects=True, vmem_limit_bytes=60 * 2**20
        ),
    )(voltages, jnp.asarray(taper_table()), jnp.asarray(spectrum_table()), station_ok.reshape(1, STATIONS), delays)
    return formed.reshape(1, FRAMES, BANDS * CHANS * KEEP)


def solution(mesh):
    placed = (P(None, "stn", None, "band", None), P(), P())
    return jax.shard_map(
        local, mesh=mesh, in_specs=placed, out_specs=P(("band", "stn"), None, None), check_vma=False
    )
```

```python
import math

import jax
import jax.numpy as jnp
import numpy as np
from jax import lax
from jax.experimental import pallas as pl
from jax.experimental.pallas import tpu as pltpu
from jax.sharding import PartitionSpec as P

STATIONS = 512
BEAMS = 512
FINE = 256
TAPS = 4
FRAMES = 3
KEEP = 192
HOP = 192
SAMP = 1408
PERIOD = 32768
MESH = pl.DeviceIdType.MESH
VMEM = pltpu.VMEM

BANDS = 4
RINGS = 16
PLANE = 8
STN = RINGS * PLANE
CHANS = 48
PER_Z = CHANS // RINGS
WORKERS = 7
LANES = 128
HALF = 64
ROWS = 2 * STATIONS
DESKS = BANDS * PLANE
SENDERS = RINGS - RINGS // PLANE


def taper_table():
    length = TAPS * FINE
    at = np.arange(length, dtype=np.float64)
    window = 0.5 - 0.5 * np.cos(2.0 * np.pi * (at + 0.5) / length)
    taper = np.sinc((at - (length - 1) / 2.0) / FINE) * window
    taper = taper / np.sqrt(np.sum(taper * taper) / FINE)
    taper = taper.reshape(TAPS, FINE)
    return np.concatenate([taper, np.pad(taper, ((0, 0), (HALF, HALF)))], axis=1).astype(np.float32)


def spectrum_table():
    n = np.arange(FINE)[:, None]
    q = (np.arange(KEEP)[None, :] - KEEP // 2) % FINE
    phase = 2.0 * np.pi * (n * q % FINE) / FINE
    both = np.stack([np.cos(phase), np.sin(phase)], axis=1) / math.sqrt(FINE)
    both = both.reshape(FINE, 2, 3, 1, HALF)
    return np.broadcast_to(both, (FINE, 2, 3, 2, HALF)).reshape(FINE, 768).astype(np.float32)


def sine_coefficients():
    x = np.cos((np.arange(400) + 0.5) * np.pi / 800) * 0.25
    powers = np.stack([x ** (2 * i + 1) for i in range(5)], axis=1)
    return [float(v) for v in np.linalg.lstsq(powers, np.sin(2 * np.pi * x), rcond=None)[0]]


SINE = sine_coefficients()


def one_hot(picked, axis, shape):
    other = lax.broadcasted_iota(jnp.int32, shape, 1 - axis)
    narrow = (8, shape[1]) if axis else (shape[0], LANES)
    picks = picked(lax.broadcasted_iota(jnp.int32, narrow, axis))
    picks = jnp.concatenate([picks] * (shape[1 - axis] // narrow[1 - axis]), axis=1 - axis)
    return jnp.where(other == picks, 1.0, 0.0).astype(jnp.bfloat16)


def dot(a, b, over=((1,), (0,))):
    return lax.dot_general(a, b, (over, ((), ())), preferred_element_type=jnp.float32)


def kernel(
    volts, taper, waves_far, station_ok, delays, out,
    held, waves, table, filtered, spectra, blocks, middle, landed, delays_in, turns, gains, spread, order, regroup, weights, formed, ordered,
    share, share_in, mine, mine_in,
    load_v, load_w, load_d, send_z, recv_z, send_x, recv_x, send_a, recv_a, send_b_sem, recv_b,
):
    band, stn = lax.axis_index("band"), lax.axis_index("stn")
    z, j = stn // PLANE, stn % PLANE
    rank = (j + 3 * PLANE - 1 - z) % PLANE
    works = rank < WORKERS
    at = band * PLANE + j
    bf16, f32 = jnp.bfloat16, jnp.float32

    barrier = pltpu.get_barrier_semaphore()

    def greet_column(i, _):
        other = (band, (z + i) % RINGS * PLANE + j)
        pl.semaphore_signal(barrier, inc=1, device_id=other, device_id_type=MESH)
        return 0

    lax.fori_loop(1, RINGS, greet_column, 0)

    def greet_plane(i, _):
        to = (at + i) % DESKS
        other = (to // PLANE, z * PLANE + to % PLANE)
        pl.semaphore_signal(barrier, inc=1, device_id=other, device_id_type=MESH)
        return 0

    lax.fori_loop(1, DESKS, greet_plane, 0)

    pltpu.make_async_copy(waves_far, waves, load_w).start()
    for s in range(4):
        pltpu.make_async_copy(volts.at[:, s], held.at[:, s], load_v.at[s]).start()
    pltpu.make_async_copy(delays, delays_in, load_d).start()

    low = lax.broadcasted_iota(jnp.int32, (64, 384), 1) % LANES < HALF

    def table_step(i, _):
        at = pl.multiple_of(i * 64, 64)
        cosine, sine = waves[pl.ds(at, 64), :384], waves[pl.ds(at, 64), 384:]
        for p in range(2):
            own = low if p == 0 else jnp.logical_not(low)
            c, s = jnp.where(own, cosine, 0.0), jnp.where(own, sine, 0.0)
            table[pl.ds(512 * p + at, 64), :384] = c.astype(bf16)
            table[pl.ds(512 * p + at, 64), 384:] = (-s).astype(bf16)
            table[pl.ds(512 * p + 256 + at, 64), :384] = s.astype(bf16)
            table[pl.ds(512 * p + 256 + at, 64), 384:] = c.astype(bf16)
        return 0

    pltpu.make_async_copy(waves_far, waves, load_w).wait()
    lax.fori_loop(0, 4, table_step, 0)

    def filter_station(s, _):
        pltpu.make_async_copy(volts.at[:, s], held.at[:, s], load_v.at[s]).wait()

        def filter_step(cb, _):
            for p in range(2):
                for r in range(2):
                    v = held[r, s, p, pl.ds(pl.multiple_of(cb * 16, 16), 16), :].astype(f32)
                    for f in range(FRAMES):
                        total = None
                        for m in range(TAPS):
                            start = f * HOP + m * FINE
                            if f == 1:
                                term = v[:, start - HALF : start + FINE + HALF] * taper[m : m + 1, FINE:]
                            else:
                                term = v[:, start : start + FINE] * taper[m : m + 1, :FINE]
                            total = term if total is None else total + term
                        if f == 1:
                            total = total[:, HALF : HALF + FINE]
                        at = pl.multiple_of((f * 3 + cb) * 64 + s * 16, 16)
                        lanes = slice((p * 2 + r) * FINE, (p * 2 + r + 1) * FINE)
                        filtered[pl.ds(at, 16), lanes] = total.astype(bf16)
            return 0

        lax.fori_loop(0, 3, filter_step, 0)
        return 0

    lax.fori_loop(0, 4, filter_station, 0)

    def transform(f):
        y = dot(filtered[f * 192 : (f + 1) * 192, :], table[...])
        for cb in range(3):
            for s in range(4):
                for part in range(6):
                    ri, g = part // 3, part % 3
                    start = ((f * CHANS + cb * 16) * 3 + g) * 8 + ri * 4 + s
                    spectra[pl.ds(start, 16, stride=24), :] = y[
                        cb * 64 + s * 16 : cb * 64 + s * 16 + 16, part * LANES : (part + 1) * LANES
                    ]

    def pack(t):
        def units(f, zz, first, last):
            start = pl.multiple_of(f * CHANS * 24 + zz * 72 + first * 8, 8)
            return spectra[pl.ds(start, (last - first) * 8), :]

        def pack_step(zz, _):
            if t == 0:
                rows = [units(0, zz, 0, 9), units(1, zz, 0, 5)]
            else:
                rows = [units(1, zz, 5, 9), units(2, zz, 0, 9), jnp.zeros((8, LANES), f32)]
            rows = jnp.concatenate(rows, axis=0).astype(bf16)
            blocks[t, zz] = rows.reshape(WORKERS, 16, LANES)
            return 0

        lax.fori_loop(0, RINGS, pack_step, 0)

    def send_along(t):
        def send_one(slot, group, zz):
            pltpu.make_async_remote_copy(
                src_ref=blocks.at[t, zz],
                dst_ref=middle.at[t, slot],
                send_sem=send_z,
                recv_sem=recv_z.at[t, group],
                device_id=(band, zz * PLANE + j),
                device_id_type=MESH,
            ).start()

        def send_two(h, _):
            for way in ((band + 0) % 2, (band + 1) % 2):
                send_one(2 * h + way, h // 2, (z + (1 + h) * (1 - 2 * way) + RINGS) % RINGS)
            return 0

        lax.fori_loop(0, RINGS // 2 - 1, send_two, 0)
        send_one(RINGS - 2, 3, (z + RINGS // 2) % RINGS)

    def pass_on(t, group, k, source, target):
        @pl.when(k == rank)
        def _():
            pltpu.make_async_copy(source, target, recv_x.at[t, group]).start()

        @pl.when(k != rank)
        def _():
            pltpu.make_async_remote_copy(
                src_ref=source,
                dst_ref=target,
                send_sem=send_x,
                recv_sem=recv_x.at[t, group],
                device_id=(band, z * PLANE + (z + 1 + k) % PLANE),
                device_id_type=MESH,
            ).start()

    def pass_own(t):
        def one(i, _):
            k = (j + i) % WORKERS
            pass_on(t, 3, k, blocks.at[t, z, k], landed.at[t, 3, j, 3])
            return 0

        lax.fori_loop(0, WORKERS, one, 0)

    def pass_group(t, group):
        count = 3 if group == 3 else 4
        slots = pl.ds(4 * group, count)
        arrived = middle.at[t, slots]
        pltpu.make_async_copy(arrived, arrived, recv_z.at[t, group]).wait()

        def one(i, _):
            k = (j + i) % WORKERS
            pass_on(t, group, k, middle.at[t, slots, k], landed.at[t, group, j, pl.ds(0, count)])
            return 0

        lax.fori_loop(0, WORKERS, one, 0)

    transform(0)
    transform(1)
    pack(0)
    pl.semaphore_wait(barrier, RINGS - 1 + DESKS - 1)
    send_along(0)
    pass_own(0)
    transform(2)
    pack(1)
    send_along(1)
    pass_own(1)

    pltpu.make_async_copy(delays, delays_in, load_d).wait()

    def station(k):
        slot = (k >> 8) * 4 + ((k >> 3) & 3)
        ahead = ((slot >> 1) + 1) * (1 - 2 * (slot & 1))
        ahead = jnp.where(slot == RINGS - 1, 0, ahead)
        return ((((z + RINGS - ahead) & 15) * PLANE) + ((k >> 5) & 7)) * 4 + (k & 3)

    spread[...] = one_hot(station, 1, (STATIONS, ROWS))
    order[...] = one_hot(lambda b: ((b >> 3) & 3) * 128 + (b >> 5) * 8 + (b & 7), 0, (BEAMS, BEAMS))
    d = delays_in[...]
    d = jnp.concatenate([d >> 8, d & 255], axis=0).astype(f32).astype(bf16)
    d = dot(order[...], d, ((1,), (1,))).astype(bf16)
    turns[...] = dot(d[:, :STATIONS], spread[...]) * 256.0 + dot(d[:, STATIONS:], spread[...])
    ok = jnp.broadcast_to(station_ok[...].astype(f32), (8, STATIONS)).astype(bf16)
    gains[...] = dot(ok, spread[...]) * (1.0 / math.sqrt(STATIONS))

    def place(k):
        after = ((k & 15) + RINGS - 1 - j) & 15
        return jnp.where((after & 7) == 7, -1, (after - (after >> 3)) * DESKS + (k >> 4))

    regroup[...] = one_hot(place, 0, (BEAMS, BEAMS))[:, : SENDERS * DESKS]

    imag = (lax.broadcasted_iota(jnp.int32, (16, ROWS), 1) >> 2) & 1
    quarter = imag.astype(f32) * -0.25
    first_channel = (band * CHANS + z * PER_Z).astype(f32)

    def weight_step(i, _):
        rows = pl.ds(pl.multiple_of(i * 16, 16), 16)
        x = turns[rows, :]
        gain = jnp.concatenate([gains[...]] * 2, axis=0)
        for c in range(PER_Z):
            turn = x * ((first_channel + float(c)) * (1.0 / PERIOD)) + quarter
            turn = turn - jnp.floor(turn + 0.5)
            a = 0.25 - jnp.abs(turn)
            square = a * a
            value = SINE[4]
            for coefficient in SINE[3::-1]:
                value = value * square + coefficient
            weights[c, rows, :] = (value * a * gain).astype(bf16)
        return 0

    for group in range(4):
        lax.fori_loop(group * 8, group * 8 + 8, weight_step, 0)
        pass_group(0, group)
    pass_group(1, 0)
    pass_group(1, 1)

    upper = lax.broadcasted_iota(jnp.int32, (1, 8, LANES), 1) < 4
    sign = jnp.where(upper, 1.0, -1.0)
    left = lax.broadcasted_iota(jnp.int32, (BEAMS, LANES), 1) < HALF

    after = (z + RINGS - 1 - j) % RINGS
    slot = after - after // PLANE

    def channel_of(t, h):
        return ((2 * (t * WORKERS + rank) + h) // 3) % 3

    def gather(t, group):
        @pl.when(works)
        def _():
            pltpu.make_async_copy(landed.at[t, group], landed.at[t, group], recv_x.at[t, group]).wait()
            x = landed[t, group].reshape(ROWS // 32, 16, LANES).astype(f32)
            for h in range(2):
                for_real = x[:, 8 * h : 8 * h + 8]
                for_imag = pltpu.roll(for_real, 4, 1) * sign
                both = [for_real.reshape(ROWS // 4, LANES), for_imag.reshape(ROWS // 4, LANES)]
                both = jnp.concatenate(both, axis=1).astype(bf16)
                y = dot(weights[channel_of(t, h), :, group * 256 : group * 256 + 256], both)
                if group == 0:
                    formed[h] = y
                else:
                    formed[h] += y

    def form(t):
        @pl.when(works)
        def _():
            powers = []
            for h in range(2):
                y = formed[h]
                y = y[:, :LANES] * y[:, :LANES] + y[:, LANES:] * y[:, LANES:]
                powers.append(y + pltpu.roll(y, HALF, 1))
            y = jnp.where(left, powers[0], powers[1]).astype(bf16)
            share[t] = y.reshape(RINGS, DESKS, LANES)

            def send_a_step(i, _, t=t):
                zz = (z + i) % RINGS
                pltpu.make_async_remote_copy(
                    src_ref=share.at[t, zz],
                    dst_ref=share_in.at[t, slot],
                    send_sem=send_a,
                    recv_sem=recv_a.at[t],
                    device_id=(band, zz * PLANE + j),
                    device_id_type=MESH,
                ).start()
                return 0

            lax.fori_loop(1, RINGS, send_a_step, 0)
            pltpu.make_async_copy(share.at[t, z], share_in.at[t, slot], recv_a.at[t]).start()

    for group in range(4):
        gather(0, group)
    form(0)
    pass_group(1, 2)
    gather(1, 0)
    gather(1, 1)
    pass_group(1, 3)
    gather(1, 2)
    gather(1, 3)
    form(1)

    for t in range(2):
        pltpu.make_async_copy(share_in.at[t], share_in.at[t], recv_a.at[t]).wait()
        moved = dot(regroup[...], share_in[t].reshape(SENDERS * DESKS, LANES))
        mine[t] = moved.astype(bf16).reshape(DESKS, RINGS, LANES)

        def send_b(i, t=t):
            to = (at + i) % DESKS
            pltpu.make_async_remote_copy(
                src_ref=mine.at[t, to],
                dst_ref=mine_in.at[t, at],
                send_sem=send_b_sem,
                recv_sem=recv_b.at[t],
                device_id=(to // PLANE, z * PLANE + to % PLANE),
                device_id_type=MESH,
            ).start()

        def send_b_step(n, _, send_b=send_b):
            for i in range(5):
                send_b(5 * n + 1 + i)
            return 0

        lax.fori_loop(0, 6, send_b_step, 0)
        send_b(DESKS - 1)
        pltpu.make_async_copy(mine.at[t, at], mine_in.at[t, at], recv_b.at[t]).start()

    width = PER_Z * KEEP
    row = lax.broadcasted_iota(jnp.int32, (RINGS, LANES), 0)

    def in_order(t, b):
        turned = [mine_in[t, b * PLANE + place].astype(f32) for place in range(PLANE)]
        for step in (1, 2, 4):
            turned = [jnp.where((row & step) > 0, turned[(i + step) % PLANE], turned[i]) for i in range(PLANE)]
        return jnp.concatenate(turned[1:], axis=1)

    pltpu.make_async_copy(mine_in.at[0], mine_in.at[0], recv_b.at[0]).wait()
    for b in range(BANDS):
        ordered[b] = in_order(0, b)
    pltpu.make_async_copy(mine_in.at[1], mine_in.at[1], recv_b.at[1]).wait()
    for b in range(BANDS):
        wide = jnp.concatenate([ordered[b], in_order(1, b)], axis=1)
        for f in range(FRAMES):
            out[f, b] = wide[:, f * width : (f + 1) * width].astype(bf16)

    some = mine.at[:, pl.ds(0, DESKS - 1)]
    pltpu.make_async_copy(some, some, send_b_sem).wait()
    some = blocks.at[:, pl.ds(0, RINGS - 1)]
    pltpu.make_async_copy(some, some, send_z).wait()

    @pl.when(works)
    def _():
        some = blocks.at[:, :, pl.ds(0, WORKERS - 1)]
        pltpu.make_async_copy(some, some, send_x).wait()
        some = share.at[:, pl.ds(0, RINGS - 1)]
        pltpu.make_async_copy(some, some, send_a).wait()

    @pl.when(jnp.logical_not(works))
    def _():
        pltpu.make_async_copy(blocks, blocks, send_x).wait()


def local(voltages, station_ok, delays):
    in_vmem, anywhere = pl.BlockSpec(memory_space=VMEM), pl.BlockSpec(memory_space=pl.ANY)
    bf16, f32 = jnp.bfloat16, jnp.float32
    dma = pltpu.SemaphoreType.DMA
    formed = pl.pallas_call(
        kernel,
        name="beams",
        out_shape=jax.ShapeDtypeStruct((FRAMES, BANDS, RINGS, PER_Z * KEEP), bf16),
        in_specs=[anywhere, in_vmem, anywhere, in_vmem, anywhere],
        out_specs=in_vmem,
        scratch_shapes=[
            VMEM((2, 4, 2, CHANS, SAMP), bf16),
            VMEM((FINE, 768), f32),
            VMEM((1024, 768), bf16),
            VMEM((FRAMES * CHANS * 4, 1024), bf16),
            VMEM((FRAMES * CHANS * 24, LANES), f32),
            VMEM((2, RINGS, WORKERS, 16, LANES), bf16),
            VMEM((2, RINGS - 1, WORKERS, 16, LANES), bf16),
            VMEM((2, 4, PLANE, 4, 16, LANES), bf16),
            VMEM((STATIONS, BEAMS), jnp.int32),
            VMEM((BEAMS, ROWS), f32),
            VMEM((8, ROWS), f32),
            VMEM((STATIONS, ROWS), bf16),
            VMEM((BEAMS, BEAMS), bf16),
            VMEM((BEAMS, SENDERS * DESKS), bf16),
            VMEM((PER_Z, BEAMS, ROWS), bf16),
            VMEM((2, BEAMS, 2 * LANES), f32),
            VMEM((BANDS, RINGS, WORKERS * LANES), f32),
            VMEM((2, RINGS, DESKS, LANES), bf16),
            VMEM((2, SENDERS, DESKS, LANES), bf16),
            VMEM((2, DESKS, RINGS, LANES), bf16),
            VMEM((2, DESKS, RINGS, LANES), bf16),
            dma((4,)), dma, dma, dma, dma((2, 4)), dma, dma((2, 4)), dma, dma((2,)), dma, dma((2,)),
        ],
        compiler_params=pltpu.CompilerParams(
            collective_id=0, has_side_effects=True, vmem_limit_bytes=60 * 2**20
        ),
    )(voltages, jnp.asarray(taper_table()), jnp.asarray(spectrum_table()), station_ok.reshape(1, STATIONS), delays)
    return formed.reshape(1, FRAMES, BANDS * CHANS * KEEP)


def solution(mesh):
    placed = (P(None, "stn", None, "band", None), P(), P())
    return jax.shard_map(
        local, mesh=mesh, in_specs=placed, out_specs=P(("band", "stn"), None, None), check_vma=False
    )
```

```python
import math

import jax
import jax.numpy as jnp
import numpy as np
from jax import lax
from jax.experimental import pallas as pl
from jax.experimental.pallas import tpu as pltpu
from jax.sharding import PartitionSpec as P

STATIONS = 512
BEAMS = 512
FINE = 256
TAPS = 4
FRAMES = 3
KEEP = 192
HOP = 192
SAMP = 1408
PERIOD = 32768
MESH = pl.DeviceIdType.MESH
VMEM = pltpu.VMEM

BANDS = 4
RINGS = 16
PLANE = 8
STN = RINGS * PLANE
CHANS = 48
PER_Z = CHANS // RINGS
WORKERS = 7
LANES = 128
HALF = 64
ROWS = 2 * STATIONS
DESKS = BANDS * PLANE
SENDERS = RINGS - RINGS // PLANE


def taper_table():
    length = TAPS * FINE
    at = np.arange(length, dtype=np.float64)
    window = 0.5 - 0.5 * np.cos(2.0 * np.pi * (at + 0.5) / length)
    taper = np.sinc((at - (length - 1) / 2.0) / FINE) * window
    taper = taper / np.sqrt(np.sum(taper * taper) / FINE)
    taper = taper.reshape(TAPS, FINE)
    return np.concatenate([taper, np.pad(taper, ((0, 0), (HALF, HALF)))], axis=1).astype(np.float32)


def spectrum_table():
    n = np.arange(FINE)[:, None]
    q = (np.arange(KEEP)[None, :] - KEEP // 2) % FINE
    phase = 2.0 * np.pi * (n * q % FINE) / FINE
    both = np.stack([np.cos(phase), np.sin(phase)], axis=1) / math.sqrt(FINE)
    both = both.reshape(FINE, 2, 3, 1, HALF)
    return np.broadcast_to(both, (FINE, 2, 3, 2, HALF)).reshape(FINE, 768).astype(np.float32)


def sine_coefficients():
    x = np.cos((np.arange(400) + 0.5) * np.pi / 800) * 0.25
    powers = np.stack([x ** (2 * i + 1) for i in range(5)], axis=1)
    return [float(v) for v in np.linalg.lstsq(powers, np.sin(2 * np.pi * x), rcond=None)[0]]


SINE = sine_coefficients()


def one_hot(picked, axis, shape):
    other = lax.broadcasted_iota(jnp.int32, shape, 1 - axis)
    narrow = (8, shape[1]) if axis else (shape[0], LANES)
    picks = picked(lax.broadcasted_iota(jnp.int32, narrow, axis))
    picks = jnp.concatenate([picks] * (shape[1 - axis] // narrow[1 - axis]), axis=1 - axis)
    return jnp.where(other == picks, 1.0, 0.0).astype(jnp.bfloat16)


def distance(h):
    return (1 + h // 2) * (1 - h % 2) + (RINGS // 2 - 1 - h // 2) * (h % 2)


def dot(a, b, over=((1,), (0,))):
    return lax.dot_general(a, b, (over, ((), ())), preferred_element_type=jnp.float32)


def kernel(
    volts, taper, waves_far, station_ok, delays, out,
    held, waves, table, filtered, spectra, blocks, middle, landed, delays_in, turns, gains, spread, order, regroup, weights, formed, ordered,
    share, share_in, mine, mine_in,
    load_v, load_w, load_d, send_z, recv_z, send_x, recv_x, send_a, recv_a, send_b_sem, recv_b,
):
    band, stn = lax.axis_index("band"), lax.axis_index("stn")
    z, j = stn // PLANE, stn % PLANE
    rank = (j + 3 * PLANE - 1 - z) % PLANE
    works = rank < WORKERS
    at = band * PLANE + j
    bf16, f32 = jnp.bfloat16, jnp.float32

    barrier = pltpu.get_barrier_semaphore()

    def greet_column(i, _):
        other = (band, (z + i) % RINGS * PLANE + j)
        pl.semaphore_signal(barrier, inc=1, device_id=other, device_id_type=MESH)
        return 0

    lax.fori_loop(1, RINGS, greet_column, 0)

    def greet_plane(i, _):
        to = (at + i) % DESKS
        other = (to // PLANE, z * PLANE + to % PLANE)
        pl.semaphore_signal(barrier, inc=1, device_id=other, device_id_type=MESH)
        return 0

    lax.fori_loop(1, DESKS, greet_plane, 0)

    pltpu.make_async_copy(waves_far, waves, load_w).start()
    for s in range(4):
        pltpu.make_async_copy(volts.at[:, s], held.at[:, s], load_v.at[s]).start()
    pltpu.make_async_copy(delays, delays_in, load_d).start()

    low = lax.broadcasted_iota(jnp.int32, (64, 384), 1) % LANES < HALF

    def table_step(i, _):
        at = pl.multiple_of(i * 64, 64)
        cosine, sine = waves[pl.ds(at, 64), :384], waves[pl.ds(at, 64), 384:]
        for p in range(2):
            own = low if p == 0 else jnp.logical_not(low)
            c, s = jnp.where(own, cosine, 0.0), jnp.where(own, sine, 0.0)
            table[pl.ds(512 * p + at, 64), :384] = c.astype(bf16)
            table[pl.ds(512 * p + at, 64), 384:] = (-s).astype(bf16)
            table[pl.ds(512 * p + 256 + at, 64), :384] = s.astype(bf16)
            table[pl.ds(512 * p + 256 + at, 64), 384:] = c.astype(bf16)
        return 0

    pltpu.make_async_copy(waves_far, waves, load_w).wait()
    lax.fori_loop(0, 4, table_step, 0)

    def filter_station(s, _):
        pltpu.make_async_copy(volts.at[:, s], held.at[:, s], load_v.at[s]).wait()

        def filter_step(cb, _):
            for p in range(2):
                for r in range(2):
                    v = held[r, s, p, pl.ds(pl.multiple_of(cb * 16, 16), 16), :].astype(f32)
                    for f in range(FRAMES):
                        total = None
                        for m in range(TAPS):
                            start = f * HOP + m * FINE
                            if f == 1:
                                term = v[:, start - HALF : start + FINE + HALF] * taper[m : m + 1, FINE:]
                            else:
                                term = v[:, start : start + FINE] * taper[m : m + 1, :FINE]
                            total = term if total is None else total + term
                        if f == 1:
                            total = total[:, HALF : HALF + FINE]
                        at = pl.multiple_of((f * 3 + cb) * 64 + s * 16, 16)
                        lanes = slice((p * 2 + r) * FINE, (p * 2 + r + 1) * FINE)
                        filtered[pl.ds(at, 16), lanes] = total.astype(bf16)
            return 0

        lax.fori_loop(0, 3, filter_step, 0)
        return 0

    lax.fori_loop(0, 4, filter_station, 0)

    def transform(f):
        y = dot(filtered[f * 192 : (f + 1) * 192, :], table[...])
        for cb in range(3):
            for s in range(4):
                for part in range(6):
                    ri, g = part // 3, part % 3
                    start = ((f * CHANS + cb * 16) * 3 + g) * 8 + ri * 4 + s
                    spectra[pl.ds(start, 16, stride=24), :] = y[
                        cb * 64 + s * 16 : cb * 64 + s * 16 + 16, part * LANES : (part + 1) * LANES
                    ]

    def pack(t):
        def units(f, zz, first, last):
            start = pl.multiple_of(f * CHANS * 24 + zz * 72 + first * 8, 8)
            return spectra[pl.ds(start, (last - first) * 8), :]

        def pack_step(zz, _):
            if t == 0:
                rows = [units(0, zz, 0, 9), units(1, zz, 0, 5)]
            else:
                rows = [units(1, zz, 5, 9), units(2, zz, 0, 9), jnp.zeros((8, LANES), f32)]
            rows = jnp.concatenate(rows, axis=0).astype(bf16)
            blocks[t, zz] = rows.reshape(WORKERS, 16, LANES)
            return 0

        lax.fori_loop(0, RINGS, pack_step, 0)

    def send_along(t):
        def send_one(slot, group, zz):
            pltpu.make_async_remote_copy(
                src_ref=blocks.at[t, zz],
                dst_ref=middle.at[t, slot],
                send_sem=send_z,
                recv_sem=recv_z.at[t, group],
                device_id=(band, zz * PLANE + j),
                device_id_type=MESH,
            ).start()

        def send_two(h, _):
            for way in (band % 2, (band + 1) % 2):
                send_one(2 * h + way, h // 2, (z + distance(h) * (1 - 2 * way) + RINGS) % RINGS)
            return 0

        lax.fori_loop(0, RINGS // 2 - 1, send_two, 0)
        send_one(RINGS - 2, 3, (z + RINGS // 2) % RINGS)

    def pass_on(t, group, k, source, target):
        @pl.when(k == rank)
        def _():
            pltpu.make_async_copy(source, target, recv_x.at[t, group]).start()

        @pl.when(k != rank)
        def _():
            pltpu.make_async_remote_copy(
                src_ref=source,
                dst_ref=target,
                send_sem=send_x,
                recv_sem=recv_x.at[t, group],
                device_id=(band, z * PLANE + (z + 1 + k) % PLANE),
                device_id_type=MESH,
            ).start()

    def pass_own(t):
        def one(i, _):
            k = (j + i) % WORKERS
            pass_on(t, 3, k, blocks.at[t, z, k], landed.at[t, 3, j, 3])
            return 0

        lax.fori_loop(0, WORKERS, one, 0)

    def pass_group(t, group):
        count = 3 if group == 3 else 4
        slots = pl.ds(4 * group, count)
        arrived = middle.at[t, slots]
        pltpu.make_async_copy(arrived, arrived, recv_z.at[t, group]).wait()

        def one(i, _):
            k = (j + i) % WORKERS
            pass_on(t, group, k, middle.at[t, slots, k], landed.at[t, group, j, pl.ds(0, count)])
            return 0

        lax.fori_loop(0, WORKERS, one, 0)

    transform(0)
    transform(1)
    pack(0)
    pl.semaphore_wait(barrier, RINGS - 1 + DESKS - 1)
    send_along(0)
    pass_own(0)
    transform(2)
    pack(1)
    send_along(1)
    pass_own(1)

    pltpu.make_async_copy(delays, delays_in, load_d).wait()

    def station(k):
        slot = (k >> 8) * 4 + ((k >> 3) & 3)
        pair = slot >> 1
        ahead = jnp.where((pair & 1) == 0, 1 + (pair >> 1), RINGS // 2 - 1 - (pair >> 1)) * (1 - 2 * (slot & 1))
        ahead = jnp.where(slot == RINGS - 2, RINGS // 2, jnp.where(slot == RINGS - 1, 0, ahead))
        return ((((z + RINGS - ahead) & 15) * PLANE) + ((k >> 5) & 7)) * 4 + (k & 3)

    spread[...] = one_hot(station, 1, (STATIONS, ROWS))
    order[...] = one_hot(lambda b: ((b >> 3) & 3) * 128 + (b >> 5) * 8 + (b & 7), 0, (BEAMS, BEAMS))
    d = delays_in[...]
    d = jnp.concatenate([d >> 8, d & 255], axis=0).astype(f32).astype(bf16)
    d = dot(order[...], d, ((1,), (1,))).astype(bf16)
    turns[...] = dot(d[:, :STATIONS], spread[...]) * 256.0 + dot(d[:, STATIONS:], spread[...])
    ok = jnp.broadcast_to(station_ok[...].astype(f32), (8, STATIONS)).astype(bf16)
    gains[...] = dot(ok, spread[...]) * (1.0 / math.sqrt(STATIONS))

    def place(k):
        after = ((k & 15) + RINGS - 1 - j) & 15
        return jnp.where((after & 7) == 7, -1, (after - (after >> 3)) * DESKS + (k >> 4))

    regroup[...] = one_hot(place, 0, (BEAMS, BEAMS))[:, : SENDERS * DESKS]

    imag = (lax.broadcasted_iota(jnp.int32, (16, ROWS), 1) >> 2) & 1
    quarter = imag.astype(f32) * -0.25
    first_channel = (band * CHANS + z * PER_Z).astype(f32)

    def weight_step(i, _):
        rows = pl.ds(pl.multiple_of(i * 16, 16), 16)
        x = turns[rows, :]
        gain = jnp.concatenate([gains[...]] * 2, axis=0)
        for c in range(PER_Z):
            turn = x * ((first_channel + float(c)) * (1.0 / PERIOD)) + quarter
            turn = turn - jnp.floor(turn + 0.5)
            a = 0.25 - jnp.abs(turn)
            square = a * a
            value = SINE[4]
            for coefficient in SINE[3::-1]:
                value = value * square + coefficient
            weights[c, rows, :] = (value * a * gain).astype(bf16)
        return 0

    for group in range(4):
        lax.fori_loop(group * 8, group * 8 + 8, weight_step, 0)
        pass_group(0, group)
    pass_group(1, 0)
    pass_group(1, 1)

    upper = lax.broadcasted_iota(jnp.int32, (1, 8, LANES), 1) < 4
    sign = jnp.where(upper, 1.0, -1.0)
    left = lax.broadcasted_iota(jnp.int32, (BEAMS, LANES), 1) < HALF

    after = (z + RINGS - 1 - j) % RINGS
    slot = after - after // PLANE

    def channel_of(t, h):
        return ((2 * (t * WORKERS + rank) + h) // 3) % 3

    def gather(t, group):
        @pl.when(works)
        def _():
            pltpu.make_async_copy(landed.at[t, group], landed.at[t, group], recv_x.at[t, group]).wait()
            x = landed[t, group].reshape(ROWS // 32, 16, LANES).astype(f32)
            for h in range(2):
                for_real = x[:, 8 * h : 8 * h + 8]
                for_imag = pltpu.roll(for_real, 4, 1) * sign
                both = [for_real.reshape(ROWS // 4, LANES), for_imag.reshape(ROWS // 4, LANES)]
                both = jnp.concatenate(both, axis=1).astype(bf16)
                y = dot(weights[channel_of(t, h), :, group * 256 : group * 256 + 256], both)
                if group == 0:
                    formed[h] = y
                else:
                    formed[h] += y

    def form(t):
        @pl.when(works)
        def _():
            powers = []
            for h in range(2):
                y = formed[h]
                y = y[:, :LANES] * y[:, :LANES] + y[:, LANES:] * y[:, LANES:]
                powers.append(y + pltpu.roll(y, HALF, 1))
            y = jnp.where(left, powers[0], powers[1]).astype(bf16)
            share[t] = y.reshape(RINGS, DESKS, LANES)

            def send_a_one(zz):
                pltpu.make_async_remote_copy(
                    src_ref=share.at[t, zz],
                    dst_ref=share_in.at[t, slot],
                    send_sem=send_a,
                    recv_sem=recv_a.at[t],
                    device_id=(band, zz * PLANE + j),
                    device_id_type=MESH,
                ).start()

            def send_a_two(h, _):
                for way in (band % 2, (band + 1) % 2):
                    send_a_one((z + distance(h) * (1 - 2 * way) + RINGS) % RINGS)
                return 0

            send_a_one((z + RINGS // 2) % RINGS)
            lax.fori_loop(0, RINGS // 2 - 1, send_a_two, 0)
            pltpu.make_async_copy(share.at[t, z], share_in.at[t, slot], recv_a.at[t]).start()

    for group in range(4):
        gather(0, group)
    form(0)
    pass_group(1, 2)
    gather(1, 0)
    gather(1, 1)
    pass_group(1, 3)
    gather(1, 2)
    gather(1, 3)
    form(1)

    for t in range(2):
        pltpu.make_async_copy(share_in.at[t], share_in.at[t], recv_a.at[t]).wait()
        moved = dot(regroup[...], share_in[t].reshape(SENDERS * DESKS, LANES))
        mine[t] = moved.astype(bf16).reshape(DESKS, RINGS, LANES)

        def send_b(i, t=t):
            to = (at + i) % DESKS
            pltpu.make_async_remote_copy(
                src_ref=mine.at[t, to],
                dst_ref=mine_in.at[t, at],
                send_sem=send_b_sem,
                recv_sem=recv_b.at[t],
                device_id=(to // PLANE, z * PLANE + to % PLANE),
                device_id_type=MESH,
            ).start()

        def send_b_step(n, _, send_b=send_b):
            for i in range(5):
                send_b(5 * n + 1 + i)
            return 0

        lax.fori_loop(0, 6, send_b_step, 0)
        send_b(DESKS - 1)
        pltpu.make_async_copy(mine.at[t, at], mine_in.at[t, at], recv_b.at[t]).start()

    width = PER_Z * KEEP
    row = lax.broadcasted_iota(jnp.int32, (RINGS, LANES), 0)

    def in_order(t, b):
        turned = [mine_in[t, b * PLANE + place].astype(f32) for place in range(PLANE)]
        for step in (1, 2, 4):
            turned = [jnp.where((row & step) > 0, turned[(i + step) % PLANE], turned[i]) for i in range(PLANE)]
        return jnp.concatenate(turned[1:], axis=1)

    pltpu.make_async_copy(mine_in.at[0], mine_in.at[0], recv_b.at[0]).wait()
    for b in range(BANDS):
        ordered[b] = in_order(0, b)
    pltpu.make_async_copy(mine_in.at[1], mine_in.at[1], recv_b.at[1]).wait()
    for b in range(BANDS):
        wide = jnp.concatenate([ordered[b], in_order(1, b)], axis=1)
        for f in range(FRAMES):
            out[f, b] = wide[:, f * width : (f + 1) * width].astype(bf16)

    some = mine.at[:, pl.ds(0, DESKS - 1)]
    pltpu.make_async_copy(some, some, send_b_sem).wait()
    some = blocks.at[:, pl.ds(0, RINGS - 1)]
    pltpu.make_async_copy(some, some, send_z).wait()

    @pl.when(works)
    def _():
        some = blocks.at[:, :, pl.ds(0, WORKERS - 1)]
        pltpu.make_async_copy(some, some, send_x).wait()
        some = share.at[:, pl.ds(0, RINGS - 1)]
        pltpu.make_async_copy(some, some, send_a).wait()

    @pl.when(jnp.logical_not(works))
    def _():
        pltpu.make_async_copy(blocks, blocks, send_x).wait()


def local(voltages, station_ok, delays):
    in_vmem, anywhere = pl.BlockSpec(memory_space=VMEM), pl.BlockSpec(memory_space=pl.ANY)
    bf16, f32 = jnp.bfloat16, jnp.float32
    dma = pltpu.SemaphoreType.DMA
    formed = pl.pallas_call(
        kernel,
        name="beams",
        out_shape=jax.ShapeDtypeStruct((FRAMES, BANDS, RINGS, PER_Z * KEEP), bf16),
        in_specs=[anywhere, in_vmem, anywhere, in_vmem, anywhere],
        out_specs=in_vmem,
        scratch_shapes=[
            VMEM((2, 4, 2, CHANS, SAMP), bf16),
            VMEM((FINE, 768), f32),
            VMEM((1024, 768), bf16),
            VMEM((FRAMES * CHANS * 4, 1024), bf16),
            VMEM((FRAMES * CHANS * 24, LANES), f32),
            VMEM((2, RINGS, WORKERS, 16, LANES), bf16),
            VMEM((2, RINGS - 1, WORKERS, 16, LANES), bf16),
            VMEM((2, 4, PLANE, 4, 16, LANES), bf16),
            VMEM((STATIONS, BEAMS), jnp.int32),
            VMEM((BEAMS, ROWS), f32),
            VMEM((8, ROWS), f32),
            VMEM((STATIONS, ROWS), bf16),
            VMEM((BEAMS, BEAMS), bf16),
            VMEM((BEAMS, SENDERS * DESKS), bf16),
            VMEM((PER_Z, BEAMS, ROWS), bf16),
            VMEM((2, BEAMS, 2 * LANES), f32),
            VMEM((BANDS, RINGS, WORKERS * LANES), f32),
            VMEM((2, RINGS, DESKS, LANES), bf16),
            VMEM((2, SENDERS, DESKS, LANES), bf16),
            VMEM((2, DESKS, RINGS, LANES), bf16),
            VMEM((2, DESKS, RINGS, LANES), bf16),
            dma((4,)), dma, dma, dma, dma((2, 4)), dma, dma((2, 4)), dma, dma((2,)), dma, dma((2,)),
        ],
        compiler_params=pltpu.CompilerParams(
            collective_id=0, has_side_effects=True, vmem_limit_bytes=60 * 2**20
        ),
    )(voltages, jnp.asarray(taper_table()), jnp.asarray(spectrum_table()), station_ok.reshape(1, STATIONS), delays)
    return formed.reshape(1, FRAMES, BANDS * CHANS * KEEP)


def solution(mesh):
    placed = (P(None, "stn", None, "band", None), P(), P())
    return jax.shard_map(
        local, mesh=mesh, in_specs=placed, out_specs=P(("band", "stn"), None, None), check_vma=False
    )
```

```python
import math

import jax
import jax.numpy as jnp
import numpy as np
from jax import lax
from jax.experimental import pallas as pl
from jax.experimental.pallas import tpu as pltpu
from jax.sharding import PartitionSpec as P

STATIONS = 512
BEAMS = 512
FINE = 256
TAPS = 4
FRAMES = 3
KEEP = 192
HOP = 192
SAMP = 1408
PERIOD = 32768
MESH = pl.DeviceIdType.MESH
VMEM = pltpu.VMEM

BANDS = 4
RINGS = 16
PLANE = 8
STN = RINGS * PLANE
CHANS = 48
PER_Z = CHANS // RINGS
WORKERS = 7
LANES = 128
HALF = 64
ROWS = 2 * STATIONS
DESKS = BANDS * PLANE
SENDERS = RINGS - RINGS // PLANE


def taper_table():
    length = TAPS * FINE
    at = np.arange(length, dtype=np.float64)
    window = 0.5 - 0.5 * np.cos(2.0 * np.pi * (at + 0.5) / length)
    taper = np.sinc((at - (length - 1) / 2.0) / FINE) * window
    taper = taper / np.sqrt(np.sum(taper * taper) / FINE)
    taper = taper.reshape(TAPS, FINE)
    return np.concatenate([taper, np.pad(taper, ((0, 0), (HALF, HALF)))], axis=1).astype(np.float32)


def spectrum_table():
    n = np.arange(FINE)[:, None]
    q = (np.arange(KEEP)[None, :] - KEEP // 2) % FINE
    phase = 2.0 * np.pi * (n * q % FINE) / FINE
    both = np.stack([np.cos(phase), np.sin(phase)], axis=1) / math.sqrt(FINE)
    both = both.reshape(FINE, 2, 3, 1, HALF)
    return np.broadcast_to(both, (FINE, 2, 3, 2, HALF)).reshape(FINE, 768).astype(np.float32)


def sine_coefficients():
    x = np.cos((np.arange(400) + 0.5) * np.pi / 800) * 0.25
    powers = np.stack([x ** (2 * i + 1) for i in range(5)], axis=1)
    return [float(v) for v in np.linalg.lstsq(powers, np.sin(2 * np.pi * x), rcond=None)[0]]


SINE = sine_coefficients()


def one_hot(picked, axis, shape):
    other = lax.broadcasted_iota(jnp.int32, shape, 1 - axis)
    narrow = (8, shape[1]) if axis else (shape[0], LANES)
    picks = picked(lax.broadcasted_iota(jnp.int32, narrow, axis))
    picks = jnp.concatenate([picks] * (shape[1 - axis] // narrow[1 - axis]), axis=1 - axis)
    return jnp.where(other == picks, 1.0, 0.0).astype(jnp.bfloat16)


def distance(h):
    return (1 + h // 2) * (1 - h % 2) + (RINGS // 2 - 1 - h // 2) * (h % 2)


def dot(a, b, over=((1,), (0,))):
    return lax.dot_general(a, b, (over, ((), ())), preferred_element_type=jnp.float32)


def kernel(
    volts, taper, waves_far, station_ok, delays, out,
    held, waves, table, filtered, spectra, blocks, middle, landed, delays_in, turns, gains, spread, order, regroup, weights, formed, ordered,
    share, share_in, mine, mine_in,
    load_v, load_w, load_d, send_z, recv_z, send_x, recv_x, send_a, recv_a, send_b_sem, recv_b,
):
    band, stn = lax.axis_index("band"), lax.axis_index("stn")
    z, j = stn // PLANE, stn % PLANE
    rank = (j + 3 * PLANE - 1 - z) % PLANE
    works = rank < WORKERS
    at = band * PLANE + j
    bf16, f32 = jnp.bfloat16, jnp.float32

    barrier = pltpu.get_barrier_semaphore()

    def greet_column(i, _):
        other = (band, (z + i) % RINGS * PLANE + j)
        pl.semaphore_signal(barrier, inc=1, device_id=other, device_id_type=MESH)
        return 0

    lax.fori_loop(1, RINGS, greet_column, 0)

    def greet_plane(i, _):
        to = (at + i) % DESKS
        other = (to // PLANE, z * PLANE + to % PLANE)
        pl.semaphore_signal(barrier, inc=1, device_id=other, device_id_type=MESH)
        return 0

    lax.fori_loop(1, DESKS, greet_plane, 0)

    pltpu.make_async_copy(waves_far, waves, load_w).start()
    for s in range(4):
        pltpu.make_async_copy(volts.at[:, s], held.at[:, s], load_v.at[s]).start()
    pltpu.make_async_copy(delays, delays_in, load_d).start()

    low = lax.broadcasted_iota(jnp.int32, (64, 384), 1) % LANES < HALF

    def table_step(i, _):
        at = pl.multiple_of(i * 64, 64)
        cosine, sine = waves[pl.ds(at, 64), :384], waves[pl.ds(at, 64), 384:]
        for p in range(2):
            own = low if p == 0 else jnp.logical_not(low)
            c, s = jnp.where(own, cosine, 0.0), jnp.where(own, sine, 0.0)
            table[pl.ds(512 * p + at, 64), :384] = c.astype(bf16)
            table[pl.ds(512 * p + at, 64), 384:] = (-s).astype(bf16)
            table[pl.ds(512 * p + 256 + at, 64), :384] = s.astype(bf16)
            table[pl.ds(512 * p + 256 + at, 64), 384:] = c.astype(bf16)
        return 0

    pltpu.make_async_copy(waves_far, waves, load_w).wait()
    lax.fori_loop(0, 4, table_step, 0)

    def filter_station(s, _):
        pltpu.make_async_copy(volts.at[:, s], held.at[:, s], load_v.at[s]).wait()

        def filter_step(cb, _):
            for p in range(2):
                for r in range(2):
                    v = held[r, s, p, pl.ds(pl.multiple_of(cb * 16, 16), 16), :].astype(f32)
                    for f in range(FRAMES):
                        total = None
                        for m in range(TAPS):
                            start = f * HOP + m * FINE
                            if f == 1:
                                term = v[:, start - HALF : start + FINE + HALF] * taper[m : m + 1, FINE:]
                            else:
                                term = v[:, start : start + FINE] * taper[m : m + 1, :FINE]
                            total = term if total is None else total + term
                        if f == 1:
                            total = total[:, HALF : HALF + FINE]
                        at = pl.multiple_of((f * 3 + cb) * 64 + s * 16, 16)
                        lanes = slice((p * 2 + r) * FINE, (p * 2 + r + 1) * FINE)
                        filtered[pl.ds(at, 16), lanes] = total.astype(bf16)
            return 0

        lax.fori_loop(0, 3, filter_step, 0)
        return 0

    lax.fori_loop(0, 4, filter_station, 0)

    def transform(f):
        y = dot(filtered[f * 192 : (f + 1) * 192, :], table[...])
        for cb in range(3):
            for s in range(4):
                for part in range(6):
                    ri, g = part // 3, part % 3
                    start = ((f * CHANS + cb * 16) * 3 + g) * 8 + ri * 4 + s
                    spectra[pl.ds(start, 16, stride=24), :] = y[
                        cb * 64 + s * 16 : cb * 64 + s * 16 + 16, part * LANES : (part + 1) * LANES
                    ]

    def pack(t):
        def units(f, zz, first, last):
            start = pl.multiple_of(f * CHANS * 24 + zz * 72 + first * 8, 8)
            return spectra[pl.ds(start, (last - first) * 8), :]

        def pack_step(zz, _):
            if t == 0:
                rows = [units(0, zz, 0, 9), units(1, zz, 0, 5)]
            else:
                rows = [units(1, zz, 5, 9), units(2, zz, 0, 9), jnp.zeros((8, LANES), f32)]
            rows = jnp.concatenate(rows, axis=0).astype(bf16)
            blocks[t, zz] = rows.reshape(WORKERS, 16, LANES)
            return 0

        lax.fori_loop(0, RINGS, pack_step, 0)

    def send_along(t):
        def send_one(slot, group, zz):
            pltpu.make_async_remote_copy(
                src_ref=blocks.at[t, zz],
                dst_ref=middle.at[t, slot],
                send_sem=send_z,
                recv_sem=recv_z.at[t, group],
                device_id=(band, zz * PLANE + j),
                device_id_type=MESH,
            ).start()

        def send_two(h, _):
            for way in (band % 2, (band + 1) % 2):
                send_one(2 * h + way, h // 2, (z + distance(h) * (1 - 2 * way) + RINGS) % RINGS)
            return 0

        lax.fori_loop(0, RINGS // 2 - 1, send_two, 0)
        send_one(RINGS - 2, 3, (z + RINGS // 2) % RINGS)

    def pass_on(t, group, k, source, target):
        @pl.when(k == rank)
        def _():
            pltpu.make_async_copy(source, target, recv_x.at[t, group]).start()

        @pl.when(k != rank)
        def _():
            pltpu.make_async_remote_copy(
                src_ref=source,
                dst_ref=target,
                send_sem=send_x,
                recv_sem=recv_x.at[t, group],
                device_id=(band, z * PLANE + (z + 1 + k) % PLANE),
                device_id_type=MESH,
            ).start()

    def pass_own(t):
        def one(i, _):
            k = (j + i) % WORKERS
            pass_on(t, 3, k, blocks.at[t, z, k], landed.at[t, 3, j, 3])
            return 0

        lax.fori_loop(0, WORKERS, one, 0)

    def pass_group(t, group):
        count = 3 if group == 3 else 4
        slots = pl.ds(4 * group, count)
        arrived = middle.at[t, slots]
        pltpu.make_async_copy(arrived, arrived, recv_z.at[t, group]).wait()

        def one(i, _):
            k = (j + i) % WORKERS
            pass_on(t, group, k, middle.at[t, slots, k], landed.at[t, group, j, pl.ds(0, count)])
            return 0

        lax.fori_loop(0, WORKERS, one, 0)

    transform(0)
    transform(1)
    pack(0)
    pl.semaphore_wait(barrier, RINGS - 1 + DESKS - 1)
    send_along(0)
    pass_own(0)
    transform(2)
    pack(1)
    send_along(1)
    pass_own(1)

    pltpu.make_async_copy(delays, delays_in, load_d).wait()

    def station(k):
        slot = (k >> 8) * 4 + ((k >> 3) & 3)
        pair = slot >> 1
        ahead = jnp.where((pair & 1) == 0, 1 + (pair >> 1), RINGS // 2 - 1 - (pair >> 1)) * (1 - 2 * (slot & 1))
        ahead = jnp.where(slot == RINGS - 2, RINGS // 2, jnp.where(slot == RINGS - 1, 0, ahead))
        return ((((z + RINGS - ahead) & 15) * PLANE) + ((k >> 5) & 7)) * 4 + (k & 3)

    spread[...] = one_hot(station, 1, (STATIONS, ROWS))
    order[...] = one_hot(lambda b: ((b >> 3) & 3) * 128 + (b >> 5) * 8 + (b & 7), 0, (BEAMS, BEAMS))
    d = delays_in[...]
    d = jnp.concatenate([d >> 8, d & 255], axis=0).astype(f32).astype(bf16)
    d = dot(order[...], d, ((1,), (1,))).astype(bf16)
    turns[...] = dot(d[:, :STATIONS], spread[...]) * 256.0 + dot(d[:, STATIONS:], spread[...])
    ok = jnp.broadcast_to(station_ok[...].astype(f32), (8, STATIONS)).astype(bf16)
    gains[...] = dot(ok, spread[...]) * (1.0 / math.sqrt(STATIONS))

    def place(k):
        after = ((k & 15) + RINGS - 1 - j) & 15
        return jnp.where((after & 7) == 7, -1, (after - (after >> 3)) * DESKS + (k >> 4))

    regroup[...] = one_hot(place, 0, (BEAMS, BEAMS))[:, : SENDERS * DESKS]

    imag = (lax.broadcasted_iota(jnp.int32, (16, ROWS), 1) >> 2) & 1
    quarter = imag.astype(f32) * -0.25
    first_channel = (band * CHANS + z * PER_Z).astype(f32)

    def weight_step(i, _):
        rows = pl.ds(pl.multiple_of(i * 16, 16), 16)
        x = turns[rows, :]
        gain = jnp.concatenate([gains[...]] * 2, axis=0)
        for c in range(PER_Z):
            turn = x * ((first_channel + float(c)) * (1.0 / PERIOD)) + quarter
            turn = turn - jnp.floor(turn + 0.5)
            a = 0.25 - jnp.abs(turn)
            square = a * a
            value = SINE[4]
            for coefficient in SINE[3::-1]:
                value = value * square + coefficient
            weights[c, rows, :] = (value * a * gain).astype(bf16)
        return 0

    for group in range(4):
        lax.fori_loop(group * 8, group * 8 + 8, weight_step, 0)
        pass_group(0, group)

    upper = lax.broadcasted_iota(jnp.int32, (1, 8, LANES), 1) < 4
    sign = jnp.where(upper, 1.0, -1.0)
    left = lax.broadcasted_iota(jnp.int32, (BEAMS, LANES), 1) < HALF

    after = (z + RINGS - 1 - j) % RINGS
    slot = after - after // PLANE

    def channel_of(t, h):
        return ((2 * (t * WORKERS + rank) + h) // 3) % 3

    def gather(t, group):
        @pl.when(works)
        def _():
            pltpu.make_async_copy(landed.at[t, group], landed.at[t, group], recv_x.at[t, group]).wait()
            x = landed[t, group].reshape(ROWS // 32, 16, LANES).astype(f32)
            for h in range(2):
                for_real = x[:, 8 * h : 8 * h + 8]
                for_imag = pltpu.roll(for_real, 4, 1) * sign
                both = [for_real.reshape(ROWS // 4, LANES), for_imag.reshape(ROWS // 4, LANES)]
                both = jnp.concatenate(both, axis=1).astype(bf16)
                y = dot(weights[channel_of(t, h), :, group * 256 : group * 256 + 256], both)
                if group == 0:
                    formed[h] = y
                else:
                    formed[h] += y

    def form(t):
        @pl.when(works)
        def _():
            powers = []
            for h in range(2):
                y = formed[h]
                y = y[:, :LANES] * y[:, :LANES] + y[:, LANES:] * y[:, LANES:]
                powers.append(y + pltpu.roll(y, HALF, 1))
            y = jnp.where(left, powers[0], powers[1]).astype(bf16)
            share[t] = y.reshape(RINGS, DESKS, LANES)

            def send_a_one(zz):
                pltpu.make_async_remote_copy(
                    src_ref=share.at[t, zz],
                    dst_ref=share_in.at[t, slot],
                    send_sem=send_a,
                    recv_sem=recv_a.at[t],
                    device_id=(band, zz * PLANE + j),
                    device_id_type=MESH,
                ).start()

            def send_a_two(h, _):
                for way in (band % 2, (band + 1) % 2):
                    send_a_one((z + distance(h) * (1 - 2 * way) + RINGS) % RINGS)
                return 0

            send_a_one((z + RINGS // 2) % RINGS)
            lax.fori_loop(0, RINGS // 2 - 1, send_a_two, 0)
            pltpu.make_async_copy(share.at[t, z], share_in.at[t, slot], recv_a.at[t]).start()

    for group in range(4):
        gather(0, group)
    form(0)
    pass_group(1, 0)
    pass_group(1, 1)
    gather(1, 0)
    pass_group(1, 2)
    gather(1, 1)
    pass_group(1, 3)
    gather(1, 2)
    gather(1, 3)
    form(1)

    for t in range(2):
        pltpu.make_async_copy(share_in.at[t], share_in.at[t], recv_a.at[t]).wait()
        moved = dot(regroup[...], share_in[t].reshape(SENDERS * DESKS, LANES))
        mine[t] = moved.astype(bf16).reshape(DESKS, RINGS, LANES)

        def send_b(i, t=t):
            to = (at + i) % DESKS
            pltpu.make_async_remote_copy(
                src_ref=mine.at[t, to],
                dst_ref=mine_in.at[t, at],
                send_sem=send_b_sem,
                recv_sem=recv_b.at[t],
                device_id=(to // PLANE, z * PLANE + to % PLANE),
                device_id_type=MESH,
            ).start()

        def send_b_step(n, _, send_b=send_b):
            for i in range(5):
                send_b(5 * n + 1 + i)
            return 0

        lax.fori_loop(0, 6, send_b_step, 0)
        send_b(DESKS - 1)
        pltpu.make_async_copy(mine.at[t, at], mine_in.at[t, at], recv_b.at[t]).start()

    width = PER_Z * KEEP
    row = lax.broadcasted_iota(jnp.int32, (RINGS, LANES), 0)

    def in_order(t, b):
        turned = [mine_in[t, b * PLANE + place].astype(f32) for place in range(PLANE)]
        for step in (1, 2, 4):
            turned = [jnp.where((row & step) > 0, turned[(i + step) % PLANE], turned[i]) for i in range(PLANE)]
        return jnp.concatenate(turned[1:], axis=1)

    pltpu.make_async_copy(mine_in.at[0], mine_in.at[0], recv_b.at[0]).wait()
    for b in range(BANDS):
        ordered[b] = in_order(0, b)
    pltpu.make_async_copy(mine_in.at[1], mine_in.at[1], recv_b.at[1]).wait()
    for b in range(BANDS):
        wide = jnp.concatenate([ordered[b], in_order(1, b)], axis=1)
        for f in range(FRAMES):
            out[f, b] = wide[:, f * width : (f + 1) * width].astype(bf16)

    some = mine.at[:, pl.ds(0, DESKS - 1)]
    pltpu.make_async_copy(some, some, send_b_sem).wait()
    some = blocks.at[:, pl.ds(0, RINGS - 1)]
    pltpu.make_async_copy(some, some, send_z).wait()

    @pl.when(works)
    def _():
        some = blocks.at[:, :, pl.ds(0, WORKERS - 1)]
        pltpu.make_async_copy(some, some, send_x).wait()
        some = share.at[:, pl.ds(0, RINGS - 1)]
        pltpu.make_async_copy(some, some, send_a).wait()

    @pl.when(jnp.logical_not(works))
    def _():
        pltpu.make_async_copy(blocks, blocks, send_x).wait()


def local(voltages, station_ok, delays):
    in_vmem, anywhere = pl.BlockSpec(memory_space=VMEM), pl.BlockSpec(memory_space=pl.ANY)
    bf16, f32 = jnp.bfloat16, jnp.float32
    dma = pltpu.SemaphoreType.DMA
    formed = pl.pallas_call(
        kernel,
        name="beams",
        out_shape=jax.ShapeDtypeStruct((FRAMES, BANDS, RINGS, PER_Z * KEEP), bf16),
        in_specs=[anywhere, in_vmem, anywhere, in_vmem, anywhere],
        out_specs=in_vmem,
        scratch_shapes=[
            VMEM((2, 4, 2, CHANS, SAMP), bf16),
            VMEM((FINE, 768), f32),
            VMEM((1024, 768), bf16),
            VMEM((FRAMES * CHANS * 4, 1024), bf16),
            VMEM((FRAMES * CHANS * 24, LANES), f32),
            VMEM((2, RINGS, WORKERS, 16, LANES), bf16),
            VMEM((2, RINGS - 1, WORKERS, 16, LANES), bf16),
            VMEM((2, 4, PLANE, 4, 16, LANES), bf16),
            VMEM((STATIONS, BEAMS), jnp.int32),
            VMEM((BEAMS, ROWS), f32),
            VMEM((8, ROWS), f32),
            VMEM((STATIONS, ROWS), bf16),
            VMEM((BEAMS, BEAMS), bf16),
            VMEM((BEAMS, SENDERS * DESKS), bf16),
            VMEM((PER_Z, BEAMS, ROWS), bf16),
            VMEM((2, BEAMS, 2 * LANES), f32),
            VMEM((BANDS, RINGS, WORKERS * LANES), f32),
            VMEM((2, RINGS, DESKS, LANES), bf16),
            VMEM((2, SENDERS, DESKS, LANES), bf16),
            VMEM((2, DESKS, RINGS, LANES), bf16),
            VMEM((2, DESKS, RINGS, LANES), bf16),
            dma((4,)), dma, dma, dma, dma((2, 4)), dma, dma((2, 4)), dma, dma((2,)), dma, dma((2,)),
        ],
        compiler_params=pltpu.CompilerParams(
            collective_id=0, has_side_effects=True, vmem_limit_bytes=60 * 2**20
        ),
    )(voltages, jnp.asarray(taper_table()), jnp.asarray(spectrum_table()), station_ok.reshape(1, STATIONS), delays)
    return formed.reshape(1, FRAMES, BANDS * CHANS * KEEP)


def solution(mesh):
    placed = (P(None, "stn", None, "band", None), P(), P())
    return jax.shard_map(
        local, mesh=mesh, in_specs=placed, out_specs=P(("band", "stn"), None, None), check_vma=False
    )
```
